128 devices in a mesh: row: 8 (over x, y_lo), col: 8 (over y_hi, z), grp: 2 (over core).
Axes of the slice: x: 4, y: 4 (y_hi: 2, y_lo: 2; y = y_hi * 2 + y_lo), z: 4, core: 2. Of those that a mesh axis runs over, the one named last changes fastest.
Arguments:
- skip: bfloat16 [128, 64, 32, 320], P('grp', 'row', 'col'), may hold values from -6 to 6
- w_up: bfloat16 [9, 320, 320], replicated, may hold values from -0.109375 to 0.109375
- w_in: bfloat16 [320, 1280], replicated, may hold values from -1.25 to 1.25
- w_out: bfloat16 [1280, 320], replicated, may hold values from -0.15625 to 0.15625
- spatial_w: bfloat16 [4, 1280, 640], replicated, may hold values from -0.5310661 to 0.5310661
- temporal_w: bfloat16 [4, 1280, 640], replicated, may hold values from -0.5310661 to 0.5310661
- grad_out: bfloat16 [128, 64, 32, 320], P('grp', 'row', 'col'), may hold values from -32 to 32
Outputs:
- grad_skip: bfloat16 [128, 64, 32, 320], P('grp', 'row', 'col')
- grad_w_up: float32 [9, 320, 320], replicated
- grad_w_in: float32 [320, 1280], replicated
- grad_w_out: float32 [1280, 320], replicated
The draws below stay inside these ranges and needn't reach their ends.
All inputs are finite; a program needn't handle non-finite values.
Results may differ from the reference program's by a relative error of at most 0.035.
Values may be sent and summed in bfloat16 or wider, within the bound.
A program may use at most 128 MiB of HBM per device.

```python
import jax
import jax.numpy as jnp
from jax import lax

C = 320
C2 = 1280
HD = 64
DA = 640
POOL = 4
TH = 8
TW = 4
FRAMES = 64
FA = 128
H = 64
W = 32
HC = 16
WC = 8
N_GRP = 2


def attention_base(key):
    base = jax.random.truncated_normal(key, -3.0, 3.0, (4, C2, DA), jnp.float32)
    factors = jnp.array([C2 ** (-0.5), C2 ** (-0.5), C2 ** (-0.5), DA ** (-0.5)], jnp.float32)
    return base * factors[:, None, None]


def draw_spatial_w(key, part):
    key = jax.random.fold_in(key, 11)
    weights = attention_base(key)
    return weights.astype(jnp.bfloat16)


def draw_temporal_w(key, part):
    key = jax.random.fold_in(key, 23)
    weights = attention_base(key)
    return weights.astype(jnp.bfloat16)


def draw_grad_out(key, part):
    key = jax.random.fold_in(key, 37)
    base = jax.random.truncated_normal(key, -4.0, 4.0, (FA, H, W, C), jnp.float32)
    frame_idx = jnp.arange(FA, dtype=jnp.int32)[:, None, None, None] // FRAMES
    row_idx = jnp.arange(H, dtype=jnp.int32)[None, :, None, None] // TH
    col_idx = jnp.arange(W, dtype=jnp.int32)[None, None, :, None] // TW
    owner = (frame_idx * (H // TH) + row_idx) * (W // TW) + col_idx
    chan_idx = jnp.arange(C, dtype=jnp.int32)[None, None, None, :]
    heavy = jnp.where(owner % C == chan_idx, 8.0, 1.0)
    return (base * heavy).astype(jnp.bfloat16)


def steps_of(rng, dims, split, least, top_value):
    loudness = 1.0
    for axis_at, shards_of in split:
        draws = jax.random.uniform(jax.random.fold_in(jax.random.fold_in(rng, 6), axis_at), (shards_of,), jnp.float32, least / len(split), top_value / len(split))
        loudness = loudness * jnp.repeat(jnp.exp(draws), dims[axis_at] // shards_of).reshape((-1,) + (1,) * (len(dims) - 1 - axis_at))
    return loudness


def scatter_about(key, shape, scale, reach, cuts=(), kind=jnp.bfloat16):
    result = jax.random.normal(key, shape, jnp.float32) * scale
    if len(cuts) > 0:
        result = steps_of(key, shape, cuts, -0.22, 0.18) * result
    return jnp.clip(result, min=-reach, max=reach).astype(kind)


def setup_inputs(seed: int = 0) -> dict:
    key_of = jax.random.split(jax.random.key(seed), 8)
    skip = scatter_about(key_of[0], (FA, H, W, C), 1.0, 6.0, ((0, 2), (1, 8), (2, 8)))
    w_up = scatter_about(key_of[1], (9, C, C), (9 * C) ** -0.5, 0.109375)
    w_in = scatter_about(key_of[2], (C, C2), (C // 16) ** -0.5, 1.25)
    w_out = scatter_about(key_of[3], (C2, C), C2 ** -0.5, 0.15625)
    spatial_w = draw_spatial_w(jax.random.fold_in(key_of[7], 71), 0)
    temporal_w = draw_temporal_w(jax.random.fold_in(key_of[7], 71), 0)
    grad_out = draw_grad_out(jax.random.fold_in(key_of[7], 71), 0)
    return dict(skip=skip, w_up=w_up, w_in=w_in, w_out=w_out, spatial_w=spatial_w, temporal_w=temporal_w, grad_out=grad_out)


def product(form, left, right):
    return jnp.einsum(form, left.astype(jnp.float32), right.astype(jnp.float32))


def project(rows, matrix):
    return jnp.dot(rows, matrix, preferred_element_type=jnp.float32)


def contract_rows(left, right):
    return lax.dot_general(left, right, (((0,), (0,)), ((), ())), preferred_element_type=jnp.float32)


def attend(inputs, weights):
    batch, count, width = inputs.shape
    heads = weights.shape[2] // HD
    flat_in = inputs.reshape(-1, width)
    queries = project(flat_in, weights[0]).astype(jnp.bfloat16).reshape(batch, count, heads, HD)
    key_rows = project(flat_in, weights[1]).astype(jnp.bfloat16).reshape(batch, count, heads, HD)
    value_rows = project(flat_in, weights[2]).astype(jnp.bfloat16).reshape(batch, count, heads, HD)
    scores = product("bqhd,bkhd->bhqk", queries, key_rows) * (HD ** -0.5)
    shifted = jnp.exp(scores - jnp.max(scores, axis=-1, keepdims=True))
    probs = shifted / jnp.sum(shifted, axis=-1, keepdims=True)
    probs_low = probs.astype(jnp.bfloat16)
    mixed = product("bhqk,bkhd->bqhd", probs_low, value_rows).astype(jnp.bfloat16)
    outputs = flat_in.astype(jnp.float32) + project(mixed.reshape(batch * count, -1), weights[3].T)
    return outputs.reshape(batch, count, width).astype(jnp.bfloat16), (queries, key_rows, value_rows, probs, probs_low)


def attend_back(cotangent, weights, saved):
    queries, key_rows, value_rows, probs, probs_low = saved
    batch, count, width = cotangent.shape
    heads = weights.shape[2] // HD
    flat_grad = cotangent.reshape(-1, width)
    grad_mixed = project(flat_grad, weights[3]).astype(jnp.bfloat16).reshape(batch, count, heads, HD)
    grad_probs = product("bqhd,bkhd->bhqk", grad_mixed, value_rows)
    grad_values = product("bhqk,bqhd->bkhd", probs_low, grad_mixed).astype(jnp.bfloat16)
    inner = jnp.sum(grad_probs * probs, axis=-1, keepdims=True)
    grad_scores = (probs * (grad_probs - inner) * (HD ** -0.5)).astype(jnp.bfloat16)
    grad_queries = product("bhqk,bkhd->bqhd", grad_scores, key_rows).astype(jnp.bfloat16)
    grad_keys = product("bhqk,bqhd->bkhd", grad_scores, queries).astype(jnp.bfloat16)
    total = flat_grad.astype(jnp.float32)
    total = total + project(grad_queries.reshape(batch * count, -1), weights[0].T)
    total = total + project(grad_keys.reshape(batch * count, -1), weights[1].T)
    total = total + project(grad_values.reshape(batch * count, -1), weights[2].T)
    return total.reshape(batch, count, width).astype(jnp.bfloat16)


def reference(skip, w_up, w_in, w_out, spatial_w, temporal_w, grad_out):
    frames_all, height, width_px, chan = skip.shape
    tokens = HC * WC
    blocks = skip.astype(jnp.float32).reshape(frames_all, HC, POOL, WC, POOL, chan)
    pooled_rows = jnp.mean(blocks, axis=(2, 4)).astype(jnp.bfloat16).reshape(frames_all * tokens, chan)
    coarse = project(pooled_rows, w_in).astype(jnp.bfloat16).reshape(frames_all, tokens, C2)
    attended, saved_space = attend(coarse, spatial_w)
    by_pixel = attended.reshape(N_GRP, FRAMES, tokens, C2).transpose(0, 2, 1, 3).reshape(N_GRP * tokens, FRAMES, C2)
    timed_pixel, saved_time = attend(by_pixel, temporal_w)
    timed = timed_pixel.reshape(N_GRP, tokens, FRAMES, C2).transpose(0, 2, 1, 3).reshape(frames_all * tokens, C2)
    expanded = project(timed, w_out).reshape(frames_all, HC, 1, WC, 1, chan)
    united = (blocks + expanded).reshape(frames_all, height, width_px, chan).astype(jnp.bfloat16)
    padding = ((0, 0), (1, 1), (1, 1), (0, 0))
    united_pad = jnp.pad(united, padding)
    grad_pad = jnp.pad(grad_out, padding)
    grad_rows = grad_out.reshape(-1, chan)
    tap_grads = []
    grad_united = jnp.zeros((frames_all * height * width_px, chan), jnp.float32)
    for tap_row in range(3):
        for tap_col in range(3):
            tap = 3 * tap_row + tap_col
            shifted_in = united_pad[:, tap_row:tap_row + height, tap_col:tap_col + width_px, :].reshape(-1, chan)
            tap_grads.append(contract_rows(shifted_in, grad_rows))
            shifted_grad = grad_pad[:, 2 - tap_row:2 - tap_row + height, 2 - tap_col:2 - tap_col + width_px, :].reshape(-1, chan)
            grad_united = grad_united + project(shifted_grad, w_up[tap].T)
    grad_w_up = jnp.stack(tap_grads)
    grad_united = grad_united.astype(jnp.bfloat16).reshape(frames_all, HC, POOL, WC, POOL, chan)
    grad_expanded = jnp.sum(grad_united.astype(jnp.float32), axis=(2, 4)).astype(jnp.bfloat16).reshape(-1, chan)
    grad_timed = project(grad_expanded, w_out.T).astype(jnp.bfloat16)
    grad_w_out = contract_rows(timed, grad_expanded)
    grad_pixel = grad_timed.reshape(N_GRP, FRAMES, tokens, C2).transpose(0, 2, 1, 3).reshape(N_GRP * tokens, FRAMES, C2)
    grad_att_pixel = attend_back(grad_pixel, temporal_w, saved_time)
    grad_attended = grad_att_pixel.reshape(N_GRP, tokens, FRAMES, C2).transpose(0, 2, 1, 3).reshape(frames_all, tokens, C2)
    grad_coarse = attend_back(grad_attended, spatial_w, saved_space).reshape(-1, C2)
    grad_pooled = project(grad_coarse, w_in.T).astype(jnp.bfloat16)
    grad_w_in = contract_rows(pooled_rows, grad_coarse)
    spread = grad_pooled.astype(jnp.float32).reshape(frames_all, HC, 1, WC, 1, chan) / (POOL * POOL)
    grad_skip = (grad_united.astype(jnp.float32) + spread).reshape(frames_all, height, width_px, chan).astype(jnp.bfloat16)
    return grad_skip, grad_w_up, grad_w_in, grad_w_out
```

```python
import jax
import jax.numpy as jnp
from jax import lax
from jax.experimental import pallas as pl
from jax.experimental.pallas import tpu as pltpu
from jax.sharding import PartitionSpec as P

HD = 64
POOL = 4
N = 8
F32 = jnp.float32
BF = jnp.bfloat16
MESH = pl.DeviceIdType.MESH


def dot(a, b):
    return lax.dot_general(a, b, (((1,), (0,)), ((), ())), preferred_element_type=F32)


def dot_nt(a, b):
    return lax.dot_general(a, b, (((1,), (1,)), ((), ())), preferred_element_type=F32)


def dot_tn(a, b):
    return lax.dot_general(a, b, (((0,), (0,)), ((), ())), preferred_element_type=F32)


def permutation(back):
    to = lax.broadcasted_iota(jnp.int32, (128, 128), 1 if back else 0)
    fro = lax.broadcasted_iota(jnp.int32, (128, 128), 0 if back else 1)
    wanted = (to % 16 // 2) * 16 + (to % 2) * 8 + to // 16
    return jnp.where(fro == wanted, 1.0, 0.0).astype(BF)


def halves():
    lane = lax.broadcasted_iota(jnp.int32, (128, 128), 1)
    low = jnp.where(lane < HD, 1.0, 0.0)
    return low.astype(BF), (1.0 - low).astype(BF), lane < HD


def lanes(pair):
    return pl.ds(pl.multiple_of(pair * 128, 128), 128)


def attend(q, k, v, probs, mixed, same_set):
    low, high, is_low = halves()

    def pair_step(pair, carry):
        cols = lanes(pair)
        q2, k2, v2 = q[:, cols], k[:, cols], v[:, cols]
        stacked = jnp.concatenate([q2 * low, q2 * high], axis=0)
        scores = dot_nt(stacked, k2) * (HD ** -0.5)
        if same_set is not None:
            scores = jnp.where(same_set, scores, -3e38)
        shifted = jnp.exp(scores - jnp.max(scores, axis=-1, keepdims=True))
        prob = shifted / jnp.sum(shifted, axis=-1, keepdims=True)
        probs[pair] = prob
        out = dot(prob.astype(BF), v2)
        mixed[:, cols] = jnp.where(is_low, out[:128], out[128:]).astype(BF)
        return carry

    lax.fori_loop(0, q.shape[1] // 128, pair_step, 0)


def attend_back(q, k, v, probs, gmix, gq, gk, gv):
    low, high, is_low = halves()

    def pair_step(pair, carry):
        cols = lanes(pair)
        q2, k2, v2, g2 = q[:, cols], k[:, cols], v[:, cols], gmix[:, cols]
        stacked = jnp.concatenate([q2 * low, q2 * high], axis=0)
        gstacked = jnp.concatenate([g2 * low, g2 * high], axis=0)
        prob = probs[pair]
        gprob = dot_nt(gstacked, v2)
        inner = jnp.sum(gprob * prob, axis=-1, keepdims=True)
        gscore = prob * (gprob - inner) * (HD ** -0.5)
        gv[:, cols] = dot_tn(prob.astype(BF), gstacked).astype(BF)
        gscore = gscore.astype(BF)
        out = dot(gscore, k2)
        gq[:, cols] = jnp.where(is_low, out[:128], out[128:]).astype(BF)
        gk[:, cols] = dot_tn(gscore, stacked).astype(BF)
        return carry

    lax.fori_loop(0, q.shape[1] // 128, pair_step, 0)


def wide_nt(base, pairs, out):
    def step(at, carry):
        cols = pl.ds(pl.multiple_of(at * 256, 256), 256)
        total = base[:, cols].astype(F32)
        for x, matrix, index in pairs:
            total = total + dot_nt(x[...], matrix[index, cols, :])
        out[:, cols] = total.astype(BF)
        return carry

    lax.fori_loop(0, out.shape[1] // 256, step, 0)


def main_kernel(
    skip_hbm, grad_hbm, wup_hbm, win_hbm, wout_hbm, sw_hbm, tw_hbm,
    out, gup, gin, gout,
    skip, gpad, wup, win, wout, sw, tw,
    a1s, a1r, a2s, a2r, b1s, b1r, b2s, b2r, c1s, c1r, c2s, c2r, d1s, d1r, d2s, d2r,
    pooled_t, coarse_t, pooled_f, coarse_f, gunited, gexp, gexp_t, gtimed, gcoarse,
    qs, ks, vs, probs_s, qt, kt, vt, probs_t, mix, mix_t, attended, timed, gmix, gq, gk, gv, gatt,
    unit_t,
    load_sem, halo_sem, swap_sem,
):
    r, c, g = lax.axis_index("row"), lax.axis_index("col"), lax.axis_index("grp")
    loads = {}
    for at, (name, src, dst) in enumerate((
        ("grad", grad_hbm, gpad.at[1:9, 1:5]),
        ("skip", skip_hbm, skip),
        ("win", win_hbm, win),
        ("wup", wup_hbm, wup),
        ("wout", wout_hbm, wout),
        ("sw", sw_hbm, sw),
        ("tw", tw_hbm, tw),
    )):
        loads[name] = pltpu.make_async_copy(src, dst, load_sem.at[at])
        loads[name].start()

    around = [(dr, dc) for dr in (-1, 0, 1) for dc in (-1, 0, 1) if (dr, dc) != (0, 0)]

    def beside(dr, dc):
        return {"row": (r + dr + N) % N, "col": (c + dc + N) % N}

    barrier = pltpu.get_barrier_semaphore()
    for d in range(1, N):
        pl.semaphore_signal(barrier, 1, device_id={"row": (r + d) % N}, device_id_type=MESH)
        pl.semaphore_signal(barrier, 1, device_id={"col": (c + d) % N}, device_id_type=MESH)
    for dr, dc in around:
        if dr != 0 and dc != 0:
            pl.semaphore_signal(barrier, 1, device_id=beside(dr, dc), device_id_type=MESH)
    pl.semaphore_wait(barrier, 2 * (N - 1) + 4)

    def send(stage, src, dst, axis, me):
        dst[me] = src[me]

        def step(d, carry):
            peer = (me + d) % N
            pltpu.make_async_remote_copy(
                src.at[peer], dst.at[me], swap_sem.at[stage, 0, peer], swap_sem.at[stage, 1, me],
                device_id={axis: peer}, device_id_type=MESH,
            ).start()
            return carry

        lax.fori_loop(1, N, step, 0)

    def arrive(stage, src, dst, axis, me):
        def step(d, carry):
            peer = (me + d) % N
            pltpu.make_async_remote_copy(
                src.at[peer], dst.at[peer], swap_sem.at[stage, 0, peer], swap_sem.at[stage, 1, peer],
                device_id={axis: peer}, device_id_type=MESH,
            ).wait()
            return carry

        lax.fori_loop(1, N, step, 0)

    def turn(src, dst, back):
        width = src.shape[2]
        rows = src[...].reshape(128, width)
        dst[...] = dot(permutation(back), rows).astype(BF).reshape(N, 16, width)

    def halo(k):
        dr, dc = around[k]
        src = gpad.at[
            {-1: pl.ds(1, 1), 0: pl.ds(1, 8), 1: pl.ds(8, 1)}[dr],
            {-1: pl.ds(1, 1), 0: pl.ds(1, 4), 1: pl.ds(4, 1)}[dc],
        ]
        dst = gpad.at[
            {-1: pl.ds(9, 1), 0: pl.ds(1, 8), 1: pl.ds(0, 1)}[dr],
            {-1: pl.ds(5, 1), 0: pl.ds(1, 4), 1: pl.ds(0, 1)}[dc],
        ]
        return pltpu.make_async_remote_copy(
            src, dst, halo_sem.at[0, k], halo_sem.at[1, k],
            device_id=beside(dr, dc), device_id_type=MESH,
        )

    loads["grad"].wait()
    for k in range(8):
        halo(k).start()

    loads["skip"].wait()
    means = []
    for p in range(2):
        total = jnp.zeros(skip.shape[2:], F32)
        for i in range(POOL):
            for j in range(POOL):
                total = total + skip[p * POOL + i, j].astype(F32)
        means.append(total * (1.0 / (POOL * POOL)))
    for f in range(N):
        rows = jnp.concatenate([means[0][8 * f:8 * f + 8], means[1][8 * f:8 * f + 8]], axis=0)
        a1s[f] = rows.astype(BF)
    pooled_t[...] = a1s[...].reshape(128, -1)
    send(0, a1s, a1r, "row", r)

    loads["win"].wait()
    coarse_t[...] = dot(pooled_t[...], win[...]).astype(BF)
    loads["wup"].wait()
    for k in range(8):
        halo(k).wait()

    @pl.when(r == 0)
    def _():
        gpad[0] = jnp.zeros(gpad.shape[1:], BF)

    @pl.when(r == N - 1)
    def _():
        gpad[9] = jnp.zeros(gpad.shape[1:], BF)

    @pl.when(c == 0)
    def _():
        gpad[:, 0] = jnp.zeros((10,) + gpad.shape[2:], BF)

    @pl.when(c == N - 1)
    def _():
        gpad[:, 5] = jnp.zeros((10,) + gpad.shape[2:], BF)

    chan = gpad.shape[3]
    gexp[...] = jnp.zeros_like(gexp)

    def back_rows(first, last):
        def step(i, carry):
            total = jnp.zeros((256, chan), F32)
            for dy in range(3):
                for dx in range(3):
                    rows = gpad[i + 2 - dy, pl.ds(2 - dx, 4)].reshape(256, chan)
                    total = total + dot_nt(rows, wup[3 * dy + dx])
            low = total.astype(BF)
            gunited[i] = low.reshape(4, 64, chan)
            gexp[i // POOL] += jnp.sum(low.astype(F32).reshape(4, 64, chan), axis=0)
            return carry

        lax.fori_loop(first, last, step, 0)

    back_rows(0, 3)
    arrive(0, a1s, a1r, "row", r)
    turn(a1r, a2s, False)
    send(1, a2s, a2r, "col", c)
    back_rows(3, 6)
    arrive(1, a2s, a2r, "col", c)
    pooled_f[...] = a2r[...].reshape(128, chan)

    coarse_f[...] = dot(pooled_f[...], win[...]).astype(BF)
    loads["sw"].wait()
    for m, ref in enumerate((qs, ks, vs)):
        ref[...] = dot(coarse_f[...], sw[m]).astype(BF)
    attend(qs, ks, vs, probs_s, mix, None)
    b1s[...] = mix[...].reshape(b1s.shape)
    send(2, b1s, b1r, "col", c)
    back_rows(6, 8)
    arrive(2, b1s, b1r, "col", c)
    turn(b1r, b2s, True)
    send(3, b2s, b2r, "row", r)
    loads["wout"].wait()
    loads["tw"].wait()
    for f in range(N):
        rows = jnp.concatenate([gexp[0, 8 * f:8 * f + 8], gexp[1, 8 * f:8 * f + 8]], axis=0)
        gexp_t[16 * f:16 * f + 16] = rows.astype(BF)
    gtimed[...] = dot(gexp_t[...], wout[...]).astype(BF)
    gmix[...] = dot(gtimed[...], tw[3]).astype(BF)
    arrive(3, b2s, b2r, "row", r)
    mix_t[...] = b2r[...].reshape(mix_t.shape)

    wide_nt(coarse_t, [(mix_t, sw, 3)], attended)
    for m, ref in enumerate((qt, kt, vt)):
        ref[...] = dot(attended[...], tw[m]).astype(BF)
    row_pixel = lax.broadcasted_iota(jnp.int32, (256, 128), 0) % 16 // 8
    key_pixel = lax.broadcasted_iota(jnp.int32, (256, 128), 1) % 16 // 8
    attend(qt, kt, vt, probs_t, mix, row_pixel == key_pixel)
    attend_back(qt, kt, vt, probs_t, gmix, gq, gk, gv)
    wide_nt(gtimed, [(gq, tw, 0), (gk, tw, 1), (gv, tw, 2)], gatt)
    c1s[...] = gatt[...].reshape(c1s.shape)
    send(4, c1s, c1r, "row", r)

    wide_nt(attended, [(mix, tw, 3)], timed)
    gout[...] = dot_tn(gexp_t[...], timed[...])
    expanded = dot_nt(timed[...], wout[...])
    for p in range(2):
        rows = jnp.concatenate(
            [expanded[16 * f + 8 * p:16 * f + 8 * p + 8] for f in range(N)], axis=0
        )

        def unite(i, carry):
            united = (skip[i].astype(F32) + rows[None]).astype(BF).reshape(256, chan)
            unit_t[:, pl.ds(pl.multiple_of(i * 256, 256), 256)] = united.T
            return carry

        lax.fori_loop(p * POOL, p * POOL + POOL, unite, 0)
    arrive(4, c1s, c1r, "row", r)
    turn(c1r, c2s, False)
    send(5, c2s, c2r, "col", c)

    def tap_step(tap, carry):
        dy, dx = tap // 3, tap % 3
        rows = gpad[pl.ds(2 - dy, 8), pl.ds(2 - dx, 4)].reshape(2048, chan)
        gup[tap] = dot(unit_t[...], rows)
        return carry

    lax.fori_loop(0, 9, tap_step, 0)
    arrive(5, c2s, c2r, "col", c)
    gatt[...] = c2r[...].reshape(gatt.shape)

    gmix[...] = dot(gatt[...], sw[3]).astype(BF)
    attend_back(qs, ks, vs, probs_s, gmix, gq, gk, gv)
    wide_nt(gatt, [(gq, sw, 0), (gk, sw, 1), (gv, sw, 2)], gcoarse)
    d1s[...] = dot_nt(gcoarse[...], win[...]).astype(BF).reshape(d1s.shape)
    send(6, d1s, d1r, "col", c)
    gin[...] = dot_tn(pooled_f[...], gcoarse[...])
    arrive(6, d1s, d1r, "col", c)
    turn(d1r, d2s, True)
    send(7, d2s, d2r, "row", r)
    arrive(7, d2s, d2r, "row", r)
    spread = d2r[...].reshape(128, chan).astype(F32) * (1.0 / (POOL * POOL))
    for p in range(2):
        rows = jnp.concatenate(
            [spread[16 * f + 8 * p:16 * f + 8 * p + 8] for f in range(N)], axis=0
        )

        def finish(i, carry):
            out[i] = (gunited[i].astype(F32) + rows[None]).astype(BF)
            return carry

        lax.fori_loop(p * POOL, p * POOL + POOL, finish, 0)


def shards(skip, w_up, w_in, w_out, spatial_w, temporal_w, grad_out):
    frames, tile_h, tile_w, chan = skip.shape
    wide = w_in.shape[1]
    att = spatial_w.shape[2]
    skip_t = jnp.transpose(skip, (1, 2, 0, 3))
    grad_t = jnp.transpose(grad_out, (1, 2, 0, 3))
    w_out_t = w_out.T

    def vm(shape, dtype=BF):
        return pltpu.VMEM(shape, dtype)

    tok = 128
    swaps = []
    for width in (chan, att, wide, chan):
        swaps += [vm((N, 16, width))] * 4
    scratch = [
        vm(skip_t.shape), vm((tile_h + 2, tile_w + 2, frames, chan)), vm(w_up.shape),
        vm(w_in.shape), vm(w_out_t.shape), vm(spatial_w.shape), vm(temporal_w.shape),
        *swaps,
        vm((tok, chan)), vm((tok, wide)), vm((tok, chan)), vm((tok, wide)),
        vm(skip_t.shape), vm((2, frames, chan), F32), vm((tok, chan)), vm((tok, wide)),
        vm((tok, wide)),
        vm((tok, att)), vm((tok, att)), vm((tok, att)), vm((att // 128, 256, 128), F32),
        vm((tok, att)), vm((tok, att)), vm((tok, att)), vm((att // 128, 256, 128), F32),
        vm((tok, att)), vm((tok, att)), vm((tok, wide)), vm((tok, wide)),
        vm((tok, att)), vm((tok, att)), vm((tok, att)), vm((tok, att)), vm((tok, wide)),
        vm((chan, frames * tile_h * tile_w)),
        pltpu.SemaphoreType.DMA((7,)), pltpu.SemaphoreType.DMA((2, 8)),
        pltpu.SemaphoreType.DMA((8, 2, N)),
    ]
    grad_skip, grad_w_up, grad_w_in, grad_w_out = pl.pallas_call(
        main_kernel,
        out_shape=(
            jax.ShapeDtypeStruct(skip_t.shape, BF),
            jax.ShapeDtypeStruct(w_up.shape, F32),
            jax.ShapeDtypeStruct(w_in.shape, F32),
            jax.ShapeDtypeStruct(w_out_t.shape, F32),
        ),
        in_specs=[pl.BlockSpec(memory_space=pl.ANY)] * 7,
        out_specs=[pl.BlockSpec(memory_space=pltpu.VMEM)] * 4,
        scratch_shapes=scratch,
        compiler_params=pltpu.CompilerParams(
            collective_id=0, has_side_effects=True, vmem_limit_bytes=60 * 1024 * 1024
        ),
        name="backward",
    )(skip_t, grad_t, w_up, w_in, w_out_t, spatial_w, temporal_w)
    grads = lax.psum((grad_w_up, grad_w_in, grad_w_out), ("row", "col", "grp"))
    return (jnp.transpose(grad_skip, (2, 0, 1, 3)), grads[0], grads[1], grads[2].T)


def solution(mesh):
    in_specs = (P("grp", "row", "col", None), P(), P(), P(), P(), P(), P("grp", "row", "col", None))
    out_specs = (P("grp", "row", "col", None), P(), P(), P())
    return jax.shard_map(shards, mesh=mesh, in_specs=in_specs, out_specs=out_specs, check_vma=False)
```

```python
import jax
import jax.numpy as jnp
from jax import lax
from jax.experimental import pallas as pl
from jax.experimental.pallas import tpu as pltpu
from jax.sharding import PartitionSpec as P

HD = 64
POOL = 4
N = 8
F32 = jnp.float32
BF = jnp.bfloat16
MESH = pl.DeviceIdType.MESH


def dot(a, b):
    return lax.dot_general(a, b, (((1,), (0,)), ((), ())), preferred_element_type=F32)


def dot_nt(a, b):
    return lax.dot_general(a, b, (((1,), (1,)), ((), ())), preferred_element_type=F32)


def dot_tn(a, b):
    return lax.dot_general(a, b, (((0,), (0,)), ((), ())), preferred_element_type=F32)


def permutation(back):
    to = lax.broadcasted_iota(jnp.int32, (128, 128), 1 if back else 0)
    fro = lax.broadcasted_iota(jnp.int32, (128, 128), 0 if back else 1)
    wanted = (to % 16 // 2) * 16 + (to % 2) * 8 + to // 16
    return jnp.where(fro == wanted, 1.0, 0.0).astype(BF)


def halves():
    lane = lax.broadcasted_iota(jnp.int32, (128, 128), 1)
    low = jnp.where(lane < HD, 1.0, 0.0)
    return low.astype(BF), (1.0 - low).astype(BF), lane < HD


def lanes(pair):
    return pl.ds(pl.multiple_of(pair * 128, 128), 128)


def attend(q, k, v, probs, mixed, same_set):
    low, high, is_low = halves()

    def pair_step(pair, carry):
        cols = lanes(pair)
        q2, k2, v2 = q[:, cols], k[:, cols], v[:, cols]
        stacked = jnp.concatenate([q2 * low, q2 * high], axis=0)
        scores = dot_nt(stacked, k2) * (HD ** -0.5)
        if same_set is not None:
            scores = jnp.where(same_set, scores, -3e38)
        shifted = jnp.exp(scores - jnp.max(scores, axis=-1, keepdims=True))
        prob = shifted / jnp.sum(shifted, axis=-1, keepdims=True)
        probs[pair] = prob
        out = dot(prob.astype(BF), v2)
        mixed[:, cols] = jnp.where(is_low, out[:128], out[128:]).astype(BF)
        return carry

    lax.fori_loop(0, q.shape[1] // 128, pair_step, 0)


def attend_back(q, k, v, probs, gmix, gq, gk, gv):
    low, high, is_low = halves()

    def pair_step(pair, carry):
        cols = lanes(pair)
        q2, k2, v2, g2 = q[:, cols], k[:, cols], v[:, cols], gmix[:, cols]
        stacked = jnp.concatenate([q2 * low, q2 * high], axis=0)
        gstacked = jnp.concatenate([g2 * low, g2 * high], axis=0)
        prob = probs[pair]
        gprob = dot_nt(gstacked, v2)
        inner = jnp.sum(gprob * prob, axis=-1, keepdims=True)
        gscore = prob * (gprob - inner) * (HD ** -0.5)
        gv[:, cols] = dot_tn(prob.astype(BF), gstacked).astype(BF)
        gscore = gscore.astype(BF)
        out = dot(gscore, k2)
        gq[:, cols] = jnp.where(is_low, out[:128], out[128:]).astype(BF)
        gk[:, cols] = dot_tn(gscore, stacked).astype(BF)
        return carry

    lax.fori_loop(0, q.shape[1] // 128, pair_step, 0)


def wide_nt(base, pairs, out):
    def step(at, carry):
        cols = pl.ds(pl.multiple_of(at * 256, 256), 256)
        total = base[:, cols].astype(F32)
        for x, matrix, index in pairs:
            total = total + dot_nt(x[...], matrix[index, cols, :])
        out[:, cols] = total.astype(BF)
        return carry

    lax.fori_loop(0, out.shape[1] // 256, step, 0)


class Sum:
    def __init__(self, place, g, blocks, paired, slots, part, slots2, own, slots3, row, fin, ring, pair):
        self.place, self.g = place, g
        self.blocks, self.paired, self.slots, self.part = blocks, paired, slots, part
        self.slots2, self.own, self.slots3, self.row, self.fin = slots2, own, slots3, row, fin
        self.ring, self.pair = ring, pair
        self.u = blocks.shape[1] // 48

    def me(self, k, stage):
        return self.place[(k + stage) % 3]

    def peer(self, k, stage, at):
        x, y, z = self.place
        axis = (k + stage) % 3
        if axis == 0:
            return {"row": at * 2 + y % 2}
        if axis == 1:
            return {"row": x * 2 + at % 2, "col": (at // 2) * 4 + z}
        return {"col": (y // 2) * 4 + at}

    def copy(self, src, dst, sem, k, stage, slot_s, slot_r, at):
        return pltpu.make_async_remote_copy(
            src, dst, self.ring.at[sem, 0, k, slot_s], self.ring.at[sem, 1, k, slot_r],
            device_id=self.peer(k, stage, at), device_id_type=MESH,
        )

    def others(self, stage, step):
        for k in range(3):
            me = self.me(k, stage)

            def one(d, carry):
                step(k, me, (me + d) % 4)
                return carry

            lax.fori_loop(1, 4, one, 0)

    def pair_copy(self):
        return pltpu.make_async_remote_copy(
            self.blocks.at[1 - self.g], self.paired, self.pair.at[0, 12], self.pair.at[1, 12],
            device_id={"grp": 1 - self.g}, device_id_type=MESH,
        )

    def pair_send(self):
        self.pair_copy().start()

    def pair_add(self):
        self.pair_copy().wait()
        size = 4 * self.u

        def step(at, carry):
            some = pl.ds(at * size, size)
            total = self.blocks[self.g, some].astype(F32) + self.paired[some].astype(F32)
            self.paired[some] = total.astype(BF)
            return carry

        lax.fori_loop(0, 12, step, 0)

    def spread_copy(self, stage, k, me, at, arriving):
        if stage == 0:
            size = 4 * self.u
            src = self.paired.at[pl.ds((4 * k + at) * size, size)]
            slots = self.slots
        else:
            src = self.part.at[k, pl.ds(at * self.u, self.u)]
            slots = self.slots2
        slot = at if arriving else me
        return self.copy(src, slots.at[k, slot], stage, k, stage, at, slot, at)

    def spread_send(self, stage):
        self.others(
            stage, lambda k, me, at: self.spread_copy(stage, k, me, at, False).start()
        )

    def spread_add(self, stage):
        self.others(
            stage, lambda k, me, at: self.spread_copy(stage, k, me, at, True).wait()
        )
        size = 4 * self.u if stage == 0 else self.u
        for k in range(3):
            me = self.me(k, stage)
            if stage == 0:
                total = self.paired[pl.ds((4 * k + me) * size, size)].astype(F32)
            else:
                total = self.part[k, pl.ds(me * size, size)].astype(F32)
            slots = self.slots if stage == 0 else self.slots2
            for d in range(1, 4):
                total = total + slots[k, (me + d) % 4].astype(F32)
            if stage == 0:
                self.part[k] = total.astype(BF)
            else:
                self.own[k] = total.astype(BF)

    def last_copy(self, k, me, at, arriving):
        slot = at if arriving else me
        return self.copy(self.own.at[k], self.slots3.at[k, slot], 2, k, 2, at, slot, at)

    def last_send(self):
        self.others(2, lambda k, me, at: self.last_copy(k, me, at, False).start())

    def last_add(self):
        self.others(2, lambda k, me, at: self.last_copy(k, me, at, True).wait())
        for k in range(3):
            self.slots3[k, self.me(k, 2)] = self.own[k]
            total = self.slots3[k, 0].astype(F32) + self.slots3[k, 1].astype(F32)
            total = total + self.slots3[k, 2].astype(F32) + self.slots3[k, 3].astype(F32)
            self.row[k, pl.ds(self.me(k, 1) * self.u, self.u)] = total.astype(BF)

    def gather_copy(self, stage, k, me, at, arriving):
        slot = at if arriving else me
        if stage == 1:
            mine = self.row.at[k, pl.ds(me * self.u, self.u)]
            dst = self.row.at[k, pl.ds(slot * self.u, self.u)]
        else:
            size = 4 * self.u
            mine = self.row.at[k]
            dst = self.fin.at[self.g, pl.ds((4 * k + slot) * size, size)]
        return self.copy(mine, dst, 4 - stage, k, stage, at, slot, at)

    def gather_send(self, stage):
        self.others(
            stage, lambda k, me, at: self.gather_copy(stage, k, me, at, False).start()
        )
        if stage == 0:
            size = 4 * self.u
            for k in range(3):
                me = self.me(k, 0)
                self.fin[self.g, pl.ds((4 * k + me) * size, size)] = self.row[k]
                self.over(k, me, True).start()

    def gather_wait(self, stage):
        def step(k, me, at):
            self.gather_copy(stage, k, me, at, True).wait()
            if stage == 0:
                self.over(k, at, True).start()

        self.others(stage, step)

    def over(self, k, at, mine):
        size = 4 * self.u
        part = self.fin.at[self.g if mine else 1 - self.g, pl.ds((4 * k + at) * size, size)]
        return pltpu.make_async_remote_copy(
            part, part, self.pair.at[0, 4 * k + at], self.pair.at[1, 4 * k + at],
            device_id={"grp": 1 - self.g}, device_id_type=MESH,
        )

    def pair_done(self):
        for k in range(3):
            for at in range(4):
                self.over(k, at, True).wait_send()
                self.over(k, at, False).wait_recv()


def main_kernel(
    skip_hbm, grad_hbm, wup_hbm, win_hbm, wout_hbm, sw_hbm, tw_hbm,
    out, fin1, fin2,
    skip, gpad, wup, win, wout, sw, tw,
    a1s, a1r, a2s, a2r, b1s, b1r, b2s, b2r, c1s, c1r, c2s, c2r, d1s, d1r, d2s, d2r,
    pooled_t, coarse_t, pooled_f, coarse_f, gunited, gexp, gexp_t, gtimed, gcoarse,
    qs, ks, vs, probs_s, qt, kt, vt, probs_t, mix, mix_t, attended, timed, gmix, gq, gk, gv, gatt,
    unit_t,
    x1, s1, z1, p1, t1, w1, v1, a1, x2, s2, z2, p2, t2, w2, v2, a2,
    load_sem, halo_sem, swap_sem, ring_sem1, pair_sem1, ring_sem2, pair_sem2,
):
    r, c, g = lax.axis_index("row"), lax.axis_index("col"), lax.axis_index("grp")
    loads = {}
    for at, (name, src, dst) in enumerate((
        ("grad", grad_hbm, gpad.at[1:9, 1:5]),
        ("skip", skip_hbm, skip),
        ("win", win_hbm, win),
        ("wup", wup_hbm, wup),
        ("wout", wout_hbm, wout),
        ("sw", sw_hbm, sw),
        ("tw", tw_hbm, tw),
    )):
        loads[name] = pltpu.make_async_copy(src, dst, load_sem.at[at])
        loads[name].start()

    around = [(dr, dc) for dr in (-1, 0, 1) for dc in (-1, 0, 1) if (dr, dc) != (0, 0)]

    def beside(dr, dc):
        return {"row": (r + dr + N) % N, "col": (c + dc + N) % N}

    barrier = pltpu.get_barrier_semaphore()
    for d in range(1, N):
        pl.semaphore_signal(barrier, 1, device_id={"row": (r + d) % N}, device_id_type=MESH)
        pl.semaphore_signal(barrier, 1, device_id={"col": (c + d) % N}, device_id_type=MESH)
    for dr, dc in around:
        if dr != 0 and dc != 0:
            pl.semaphore_signal(barrier, 1, device_id=beside(dr, dc), device_id_type=MESH)
    x, y, z = r // 2, (c // 4) * 2 + r % 2, c % 4
    pl.semaphore_signal(
        barrier, 1, device_id={"row": x * 2 + (r + 1) % 2, "col": (c + 4) % N}, device_id_type=MESH
    )
    pl.semaphore_signal(barrier, 1, device_id={"grp": 1 - g}, device_id_type=MESH)
    pl.semaphore_wait(barrier, 2 * (N - 1) + 6)
    first = Sum((x, y, z), g, x1, s1, z1, p1, t1, w1, v1, a1, fin1, ring_sem1, pair_sem1)
    second = Sum((x, y, z), g, x2, s2, z2, p2, t2, w2, v2, a2, fin2, ring_sem2, pair_sem2)

    def send(stage, src, dst, axis, me):
        dst[me] = src[me]

        def step(d, carry):
            peer = (me + d) % N
            pltpu.make_async_remote_copy(
                src.at[peer], dst.at[me], swap_sem.at[stage, 0, peer], swap_sem.at[stage, 1, me],
                device_id={axis: peer}, device_id_type=MESH,
            ).start()
            return carry

        lax.fori_loop(1, N, step, 0)

    def arrive(stage, src, dst, axis, me):
        def step(d, carry):
            peer = (me + d) % N
            pltpu.make_async_remote_copy(
                src.at[peer], dst.at[peer], swap_sem.at[stage, 0, peer], swap_sem.at[stage, 1, peer],
                device_id={axis: peer}, device_id_type=MESH,
            ).wait()
            return carry

        lax.fori_loop(1, N, step, 0)

    def turn(src, dst, back):
        width = src.shape[2]
        rows = src[...].reshape(128, width)
        dst[...] = dot(permutation(back), rows).astype(BF).reshape(N, 16, width)

    def halo(k):
        dr, dc = around[k]
        src = gpad.at[
            {-1: pl.ds(1, 1), 0: pl.ds(1, 8), 1: pl.ds(8, 1)}[dr],
            {-1: pl.ds(1, 1), 0: pl.ds(1, 4), 1: pl.ds(4, 1)}[dc],
        ]
        dst = gpad.at[
            {-1: pl.ds(9, 1), 0: pl.ds(1, 8), 1: pl.ds(0, 1)}[dr],
            {-1: pl.ds(5, 1), 0: pl.ds(1, 4), 1: pl.ds(0, 1)}[dc],
        ]
        return pltpu.make_async_remote_copy(
            src, dst, halo_sem.at[0, k], halo_sem.at[1, k],
            device_id=beside(dr, dc), device_id_type=MESH,
        )

    loads["grad"].wait()
    for k in range(8):
        halo(k).start()
    x1[0, 140:144] = jnp.zeros((4,) + x1.shape[2:], BF)
    x1[1, 120:144] = jnp.zeros((24,) + x1.shape[2:], BF)
    for half in range(2):
        x2[half, 40:48] = jnp.zeros((8,) + x2.shape[2:], BF)

    loads["skip"].wait()
    means = []
    for p in range(2):
        total = jnp.zeros(skip.shape[2:], F32)
        for i in range(POOL):
            for j in range(POOL):
                total = total + skip[p * POOL + i, j].astype(F32)
        means.append(total * (1.0 / (POOL * POOL)))
    for f in range(N):
        rows = jnp.concatenate([means[0][8 * f:8 * f + 8], means[1][8 * f:8 * f + 8]], axis=0)
        a1s[f] = rows.astype(BF)
    pooled_t[...] = a1s[...].reshape(128, -1)
    send(0, a1s, a1r, "row", r)

    loads["win"].wait()
    coarse_t[...] = dot(pooled_t[...], win[...]).astype(BF)
    loads["wup"].wait()
    for k in range(8):
        halo(k).wait()

    @pl.when(r == 0)
    def _():
        gpad[0] = jnp.zeros(gpad.shape[1:], BF)

    @pl.when(r == N - 1)
    def _():
        gpad[9] = jnp.zeros(gpad.shape[1:], BF)

    @pl.when(c == 0)
    def _():
        gpad[:, 0] = jnp.zeros((10,) + gpad.shape[2:], BF)

    @pl.when(c == N - 1)
    def _():
        gpad[:, 5] = jnp.zeros((10,) + gpad.shape[2:], BF)

    chan = gpad.shape[3]
    gexp[...] = jnp.zeros_like(gexp)

    def back_rows(first, last):
        def step(i, carry):
            total = jnp.zeros((256, chan), F32)
            for dy in range(3):
                for dx in range(3):
                    rows = gpad[i + 2 - dy, pl.ds(2 - dx, 4)].reshape(256, chan)
                    total = total + dot_nt(rows, wup[3 * dy + dx])
            low = total.astype(BF)
            gunited[i] = low.reshape(4, 64, chan)
            gexp[i // POOL] += jnp.sum(low.astype(F32).reshape(4, 64, chan), axis=0)
            return carry

        lax.fori_loop(first, last, step, 0)

    back_rows(0, 3)
    arrive(0, a1s, a1r, "row", r)
    turn(a1r, a2s, False)
    send(1, a2s, a2r, "col", c)
    back_rows(3, 6)
    arrive(1, a2s, a2r, "col", c)
    pooled_f[...] = a2r[...].reshape(128, chan)

    coarse_f[...] = dot(pooled_f[...], win[...]).astype(BF)
    loads["sw"].wait()
    for m, ref in enumerate((qs, ks, vs)):
        ref[...] = dot(coarse_f[...], sw[m]).astype(BF)
    attend(qs, ks, vs, probs_s, mix, None)
    b1s[...] = mix[...].reshape(b1s.shape)
    send(2, b1s, b1r, "col", c)
    back_rows(6, 8)
    arrive(2, b1s, b1r, "col", c)
    turn(b1r, b2s, True)
    send(3, b2s, b2r, "row", r)
    loads["wout"].wait()
    loads["tw"].wait()
    for f in range(N):
        rows = jnp.concatenate([gexp[0, 8 * f:8 * f + 8], gexp[1, 8 * f:8 * f + 8]], axis=0)
        gexp_t[16 * f:16 * f + 16] = rows.astype(BF)
    gtimed[...] = dot(gexp_t[...], wout[...]).astype(BF)
    gmix[...] = dot(gtimed[...], tw[3]).astype(BF)
    arrive(3, b2s, b2r, "row", r)
    mix_t[...] = b2r[...].reshape(mix_t.shape)

    wide_nt(coarse_t, [(mix_t, sw, 3)], attended)
    for m, ref in enumerate((qt, kt, vt)):
        ref[...] = dot(attended[...], tw[m]).astype(BF)
    row_pixel = lax.broadcasted_iota(jnp.int32, (256, 128), 0) % 16 // 8
    key_pixel = lax.broadcasted_iota(jnp.int32, (256, 128), 1) % 16 // 8
    attend(qt, kt, vt, probs_t, mix, row_pixel == key_pixel)
    attend_back(qt, kt, vt, probs_t, gmix, gq, gk, gv)
    wide_nt(gtimed, [(gq, tw, 0), (gk, tw, 1), (gv, tw, 2)], gatt)
    c1s[...] = gatt[...].reshape(c1s.shape)
    send(4, c1s, c1r, "row", r)

    wide_nt(attended, [(mix, tw, 3)], timed)
    for k in range(4):
        part = dot_tn(gexp_t[...], timed[:, k * chan:(k + 1) * chan])
        x1[1, 40 + 20 * k:60 + 20 * k] = part.astype(BF).reshape(20, 16, chan)
    expanded = dot_nt(timed[...], wout[...])
    for p in range(2):
        rows = jnp.concatenate(
            [expanded[16 * f + 8 * p:16 * f + 8 * p + 8] for f in range(N)], axis=0
        )

        def unite(i, carry):
            united = (skip[i].astype(F32) + rows[None]).astype(BF).reshape(256, chan)
            unit_t[:, pl.ds(pl.multiple_of(i * 256, 256), 256)] = united.T
            return carry

        lax.fori_loop(p * POOL, p * POOL + POOL, unite, 0)
    arrive(4, c1s, c1r, "row", r)
    turn(c1r, c2s, False)
    send(5, c2s, c2r, "col", c)

    def tap_step(tap, carry):
        dy, dx = tap // 3, tap % 3
        rows = gpad[pl.ds(2 - dy, 8), pl.ds(2 - dx, 4)].reshape(2048, chan)
        owner = tap // 7
        x1[owner, pl.ds(20 * (tap - 7 * owner), 20)] = (
            dot(unit_t[...], rows).astype(BF).reshape(20, 16, chan)
        )
        return carry

    lax.fori_loop(0, 9, tap_step, 0)
    first.pair_send()
    arrive(5, c2s, c2r, "col", c)
    gatt[...] = c2r[...].reshape(gatt.shape)

    gmix[...] = dot(gatt[...], sw[3]).astype(BF)
    first.pair_add()
    first.spread_send(0)
    attend_back(qs, ks, vs, probs_s, gmix, gq, gk, gv)
    first.spread_add(0)
    first.spread_send(1)
    wide_nt(gatt, [(gq, sw, 0), (gk, sw, 1), (gv, sw, 2)], gcoarse)
    d1s[...] = dot_nt(gcoarse[...], win[...]).astype(BF).reshape(d1s.shape)
    send(6, d1s, d1r, "col", c)
    first.spread_add(1)
    first.last_send()
    for k in range(4):
        part = dot_tn(pooled_f[...], gcoarse[:, k * chan:(k + 1) * chan])
        x2[k // 2, 20 * (k % 2):20 * (k % 2) + 20] = part.astype(BF).reshape(20, 16, chan)
    second.pair_send()
    arrive(6, d1s, d1r, "col", c)
    turn(d1r, d2s, True)
    send(7, d2s, d2r, "row", r)
    first.last_add()
    first.gather_send(1)
    second.pair_add()
    second.spread_send(0)
    first.gather_wait(1)
    first.gather_send(0)
    arrive(7, d2s, d2r, "row", r)
    spread = d2r[...].reshape(128, chan).astype(F32) * (1.0 / (POOL * POOL))
    for p in range(2):
        rows = jnp.concatenate(
            [spread[16 * f + 8 * p:16 * f + 8 * p + 8] for f in range(N)], axis=0
        )

        def finish(i, carry):
            out[i] = (gunited[i].astype(F32) + rows[None]).astype(BF)
            return carry

        lax.fori_loop(p * POOL, p * POOL + POOL, finish, 0)
    second.spread_add(0)
    second.spread_send(1)
    first.gather_wait(0)
    second.spread_add(1)
    second.last_send()
    second.last_add()
    second.gather_send(1)
    second.gather_wait(1)
    second.gather_send(0)
    second.gather_wait(0)
    first.pair_done()
    second.pair_done()


def shards(skip, w_up, w_in, w_out, spatial_w, temporal_w, grad_out):
    frames, tile_h, tile_w, chan = skip.shape
    wide = w_in.shape[1]
    att = spatial_w.shape[2]
    skip_t = jnp.transpose(skip, (1, 2, 0, 3))
    grad_t = jnp.transpose(grad_out, (1, 2, 0, 3))
    w_out_t = w_out.T

    def vm(shape, dtype=BF):
        return pltpu.VMEM(shape, dtype)

    tok = 128
    swaps = []
    for width in (chan, att, wide, chan):
        swaps += [vm((N, 16, width))] * 4

    def sums(u):
        block = (16, chan)
        return [
            vm((2, 48 * u) + block), vm((48 * u,) + block), vm((3, 4, 4 * u) + block),
            vm((3, 4 * u) + block), vm((3, 4, u) + block), vm((3, u) + block),
            vm((3, 4, u) + block), vm((3, 4 * u) + block),
        ]

    scratch = [
        vm(skip_t.shape), vm((tile_h + 2, tile_w + 2, frames, chan)), vm(w_up.shape),
        vm(w_in.shape), vm(w_out_t.shape), vm(spatial_w.shape), vm(temporal_w.shape),
        *swaps,
        vm((tok, chan)), vm((tok, wide)), vm((tok, chan)), vm((tok, wide)),
        vm(skip_t.shape), vm((2, frames, chan), F32), vm((tok, chan)), vm((tok, wide)),
        vm((tok, wide)),
        vm((tok, att)), vm((tok, att)), vm((tok, att)), vm((att // 128, 256, 128), F32),
        vm((tok, att)), vm((tok, att)), vm((tok, att)), vm((att // 128, 256, 128), F32),
        vm((tok, att)), vm((tok, att)), vm((tok, wide)), vm((tok, wide)),
        vm((tok, att)), vm((tok, att)), vm((tok, att)), vm((tok, att)), vm((tok, wide)),
        vm((chan, frames * tile_h * tile_w)),
        *sums(3), *sums(1),
        pltpu.SemaphoreType.DMA((7,)), pltpu.SemaphoreType.DMA((2, 8)),
        pltpu.SemaphoreType.DMA((8, 2, N)),
        *[pltpu.SemaphoreType.DMA((5, 2, 3, 4)), pltpu.SemaphoreType.DMA((2, 13))] * 2,
    ]
    grad_skip, sum1, sum2 = pl.pallas_call(
        main_kernel,
        out_shape=(
            jax.ShapeDtypeStruct(skip_t.shape, BF),
            jax.ShapeDtypeStruct((2, 144, 16, chan), BF),
            jax.ShapeDtypeStruct((2, 48, 16, chan), BF),
        ),
        in_specs=[pl.BlockSpec(memory_space=pl.ANY)] * 7,
        out_specs=[pl.BlockSpec(memory_space=pltpu.VMEM)] * 3,
        scratch_shapes=scratch,
        compiler_params=pltpu.CompilerParams(
            collective_id=0, has_side_effects=True, vmem_limit_bytes=60 * 1024 * 1024
        ),
        name="backward",
    )(skip_t, grad_t, w_up, w_in, w_out_t, spatial_w, temporal_w)
    up = jnp.concatenate([sum1[0, :140], sum1[1, :40]], axis=0).reshape(w_up.shape).astype(F32)

    def wide_of(blocks):
        return jnp.swapaxes(blocks.reshape(4, chan, chan), 0, 1).reshape(chan, wide).astype(F32)

    grad_w_out = wide_of(sum1[1, 40:120]).T
    grad_w_in = wide_of(jnp.concatenate([sum2[0, :40], sum2[1, :40]], axis=0))
    return (jnp.transpose(grad_skip, (2, 0, 1, 3)), up, grad_w_in, grad_w_out)


def solution(mesh):
    in_specs = (P("grp", "row", "col", None), P(), P(), P(), P(), P(), P("grp", "row", "col", None))
    out_specs = (P("grp", "row", "col", None), P(), P(), P())
    return jax.shard_map(shards, mesh=mesh, in_specs=in_specs, out_specs=out_specs, check_vma=False)
```

```python
import jax
import jax.numpy as jnp
from jax import lax
from jax.experimental import pallas as pl
from jax.experimental.pallas import tpu as pltpu
from jax.sharding import PartitionSpec as P

HD = 64
POOL = 4
N = 8
F32 = jnp.float32
BF = jnp.bfloat16
MESH = pl.DeviceIdType.MESH
SIZES1 = (7, 7, 7)
SIZES2 = (3, 2, 2)


def dot(a, b):
    return lax.dot_general(a, b, (((1,), (0,)), ((), ())), preferred_element_type=F32)


def dot_nt(a, b):
    return lax.dot_general(a, b, (((1,), (1,)), ((), ())), preferred_element_type=F32)


def dot_tn(a, b):
    return lax.dot_general(a, b, (((0,), (0,)), ((), ())), preferred_element_type=F32)


def permutation(back):
    to = lax.broadcasted_iota(jnp.int32, (128, 128), 1 if back else 0)
    fro = lax.broadcasted_iota(jnp.int32, (128, 128), 0 if back else 1)
    wanted = (to % 16 // 2) * 16 + (to % 2) * 8 + to // 16
    return jnp.where(fro == wanted, 1.0, 0.0).astype(BF)


def halves():
    lane = lax.broadcasted_iota(jnp.int32, (128, 128), 1)
    low = jnp.where(lane < HD, 1.0, 0.0)
    return low.astype(BF), (1.0 - low).astype(BF), lane < HD


def lanes(pair):
    return pl.ds(pl.multiple_of(pair * 128, 128), 128)


def attend(q, k, v, probs, mixed, same_set):
    low, high, is_low = halves()

    def pair_step(pair, carry):
        cols = lanes(pair)
        q2, k2, v2 = q[:, cols], k[:, cols], v[:, cols]
        stacked = jnp.concatenate([q2 * low, q2 * high], axis=0)
        scores = dot_nt(stacked, k2) * (HD ** -0.5)
        if same_set is not None:
            scores = jnp.where(same_set, scores, -3e38)
        shifted = jnp.exp(scores - jnp.max(scores, axis=-1, keepdims=True))
        prob = shifted / jnp.sum(shifted, axis=-1, keepdims=True)
        probs[pair] = prob
        out = dot(prob.astype(BF), v2)
        mixed[:, cols] = jnp.where(is_low, out[:128], out[128:]).astype(BF)
        return carry

    lax.fori_loop(0, q.shape[1] // 128, pair_step, 0)


def attend_back(q, k, v, probs, gmix, gq, gk, gv):
    low, high, is_low = halves()

    def pair_step(pair, carry):
        cols = lanes(pair)
        q2, k2, v2, g2 = q[:, cols], k[:, cols], v[:, cols], gmix[:, cols]
        stacked = jnp.concatenate([q2 * low, q2 * high], axis=0)
        gstacked = jnp.concatenate([g2 * low, g2 * high], axis=0)
        prob = probs[pair]
        gprob = dot_nt(gstacked, v2)
        inner = jnp.sum(gprob * prob, axis=-1, keepdims=True)
        gscore = prob * (gprob - inner) * (HD ** -0.5)
        gv[:, cols] = dot_tn(prob.astype(BF), gstacked).astype(BF)
        gscore = gscore.astype(BF)
        out = dot(gscore, k2)
        gq[:, cols] = jnp.where(is_low, out[:128], out[128:]).astype(BF)
        gk[:, cols] = dot_tn(gscore, stacked).astype(BF)
        return carry

    lax.fori_loop(0, q.shape[1] // 128, pair_step, 0)


def wide_nt(base, pairs, out):
    def step(at, carry):
        cols = pl.ds(pl.multiple_of(at * 256, 256), 256)
        total = base[:, cols].astype(F32)
        for x, matrix, index in pairs:
            total = total + dot_nt(x[...], matrix[index, cols, :])
        out[:, cols] = total.astype(BF)
        return carry

    lax.fori_loop(0, out.shape[1] // 256, step, 0)


def put(units, group, product):
    for n in range(product.shape[1] // 128):
        part = product[:, 128 * n:128 * n + 128].astype(BF).reshape(-1, 16, 128)
        size = part.shape[0]
        units[pl.ds((group + n) * size, size)] = part


def wide_tn(left, right, units, group):
    def step(at, carry):
        cols = pl.ds(pl.multiple_of(at * 256, 256), 256)
        put(units, group + 2 * at, dot_tn(left[...], right[:, cols]))
        return carry

    lax.fori_loop(0, right.shape[1] // 256, step, 0)


class Sum:
    def __init__(self, place, g, sizes, blocks, paired, slots, part, slots2, own, slots3, row, fin,
                 ring, pair):
        self.place, self.g, self.sizes = place, g, sizes
        self.blocks, self.paired, self.slots, self.part = blocks, paired, slots, part
        self.slots2, self.own, self.slots3, self.row, self.fin = slots2, own, slots3, row, fin
        self.ring, self.pair = ring, pair
        self.offs = [sum(sizes[:k]) for k in range(3)]
        self.total = 16 * sum(sizes)

    def big(self, k, at, base=0):
        return pl.ds(base + 16 * self.offs[k] + at * (4 * self.sizes[k]), 4 * self.sizes[k])

    def small(self, k, at):
        return pl.ds(4 * self.offs[k] + at * self.sizes[k], self.sizes[k])

    def line(self, k):
        return pl.ds(4 * self.offs[k], 4 * self.sizes[k])

    def mine(self, k):
        return pl.ds(self.offs[k], self.sizes[k])

    def me(self, k, stage):
        return self.place[(k + stage) % 3]

    def peer(self, k, stage, at):
        x, y, z = self.place
        axis = (k + stage) % 3
        if axis == 0:
            return {"row": at * 2 + y % 2}
        if axis == 1:
            return {"row": x * 2 + at % 2, "col": (at // 2) * 4 + z}
        return {"col": (y // 2) * 4 + at}

    def copy(self, src, dst, sem, k, stage, slot_s, slot_r, at):
        return pltpu.make_async_remote_copy(
            src, dst, self.ring.at[sem, 0, k, slot_s], self.ring.at[sem, 1, k, slot_r],
            device_id=self.peer(k, stage, at), device_id_type=MESH,
        )

    def others(self, stage, step):
        for k in range(3):
            me = self.me(k, stage)

            def one(d, carry):
                step(k, me, (me + d) % 4)
                return carry

            lax.fori_loop(1, 4, one, 0)

    def quarters(self, step):
        for k in range(3):
            def one(at, carry):
                step(k, at)
                return carry

            lax.fori_loop(0, 4, one, 0)

    def pair_copy(self, k, at):
        return pltpu.make_async_remote_copy(
            self.blocks.at[self.big(k, at, (1 - self.g) * self.total)],
            self.paired.at[self.big(k, at)],
            self.pair.at[0, 0, 4 * k + at], self.pair.at[0, 1, 4 * k + at],
            device_id={"grp": 1 - self.g}, device_id_type=MESH,
        )

    def pair_send(self):
        self.quarters(lambda k, at: self.pair_copy(k, at).start())

    def pair_add(self):
        def step(k, at):
            self.pair_copy(k, at).wait()
            some = self.big(k, at)
            total = self.blocks[self.big(k, at, self.g * self.total)].astype(F32)
            self.paired[some] = (total + self.paired[some].astype(F32)).astype(BF)

        self.quarters(step)

    def spread_copy(self, stage, k, me, at, arriving):
        slot = at if arriving else me
        if stage == 0:
            src, dst = self.paired.at[self.big(k, at)], self.slots.at[self.big(k, slot)]
        else:
            src, dst = self.part.at[self.small(k, at)], self.slots2.at[self.small(k, slot)]
        return self.copy(src, dst, stage, k, stage, at, slot, at)

    def spread_send(self, stage):
        self.others(
            stage, lambda k, me, at: self.spread_copy(stage, k, me, at, False).start()
        )

    def spread_add(self, stage):
        for k in range(3):
            me = self.me(k, stage)

            def one(d, carry):
                self.spread_copy(stage, k, me, (me + d) % 4, True).wait()
                return carry

            lax.fori_loop(1, 4, one, 0)
            if stage == 0:
                total = self.paired[self.big(k, me)].astype(F32)
                for d in range(1, 4):
                    total = total + self.slots[self.big(k, (me + d) % 4)].astype(F32)
                self.part[self.line(k)] = total.astype(BF)
            else:
                total = self.part[self.small(k, me)].astype(F32)
                for d in range(1, 4):
                    total = total + self.slots2[self.small(k, (me + d) % 4)].astype(F32)
                self.own[self.mine(k)] = total.astype(BF)

    def last_copy(self, k, me, at, arriving):
        slot = at if arriving else me
        dst = self.slots3.at[self.small(k, slot)]
        return self.copy(self.own.at[self.mine(k)], dst, 2, k, 2, at, slot, at)

    def last_send(self):
        self.others(2, lambda k, me, at: self.last_copy(k, me, at, False).start())

    def last_add(self):
        self.others(2, lambda k, me, at: self.last_copy(k, me, at, True).wait())
        for k in range(3):
            self.slots3[self.small(k, self.me(k, 2))] = self.own[self.mine(k)]
            total = self.slots3[self.small(k, 0)].astype(F32)
            for at in range(1, 4):
                total = total + self.slots3[self.small(k, at)].astype(F32)
            self.row[self.small(k, self.me(k, 1))] = total.astype(BF)

    def gather_copy(self, stage, k, me, at, arriving):
        slot = at if arriving else me
        if stage == 1:
            src, dst = self.row.at[self.small(k, me)], self.row.at[self.small(k, slot)]
        else:
            src = self.row.at[self.line(k)]
            dst = self.fin.at[self.big(k, slot, self.g * self.total)]
        return self.copy(src, dst, 4 - stage, k, stage, at, slot, at)

    def gather_send(self, stage):
        self.others(
            stage, lambda k, me, at: self.gather_copy(stage, k, me, at, False).start()
        )
        if stage == 0:
            for k in range(3):
                me = self.me(k, 0)
                self.fin[self.big(k, me, self.g * self.total)] = self.row[self.line(k)]
                self.over(k, me, True).start()

    def gather_wait(self, stage):
        def step(k, me, at):
            self.gather_copy(stage, k, me, at, True).wait()
            if stage == 0:
                self.over(k, at, True).start()

        self.others(stage, step)

    def over(self, k, at, mine):
        half = self.g if mine else 1 - self.g
        part = self.fin.at[self.big(k, at, half * self.total)]
        return pltpu.make_async_remote_copy(
            part, part, self.pair.at[1, 0, 4 * k + at], self.pair.at[1, 1, 4 * k + at],
            device_id={"grp": 1 - self.g}, device_id_type=MESH,
        )

    def pair_done(self):
        def step(k, at):
            self.over(k, at, True).wait_send()
            self.over(k, at, False).wait_recv()

        self.quarters(step)


class Loads:
    def __init__(self, copies):
        self.copies = copies

    def start(self):
        for copy in self.copies:
            copy.start()

    def wait(self):
        for copy in self.copies:
            copy.wait()


def cut_rows(ref, count):
    size = ref.shape[1] // count
    return [pl.ds(size * n, size) for n in range(count)]


def main_kernel(
    skip_hbm, grad_hbm, wup_hbm, win_hbm, wout_hbm, sw_hbm, tw_hbm,
    out, up_out, wide_out,
    skip, gpad, wup, win, wout, sw, tw,
    a1s, a1r, a2s, a2r, b1s, b1r, b2s, b2r, c1s, c1r, c2s, c2r, d1s, d1r, d2s, d2r,
    pooled_t, coarse_t, pooled_f, coarse_f, gunited, gexp, gexp_t, gtimed, gcoarse,
    qs, ks, vs, probs_s, qt, kt, vt, probs_t, mix, mix_t, attended, timed, gmix, gq, gk, gv, gatt,
    unit_t,
    x1, s1, z1, p1, t1, w1, v1, a1, fin1, x2, s2, z2, p2, t2, w2, v2, a2, fin2,
    load_sem, halo_sem, swap_sem, ring_sem1, pair_sem1, ring_sem2, pair_sem2,
):
    r, c, g = lax.axis_index("row"), lax.axis_index("col"), lax.axis_index("grp")
    loads = {}
    load_at = 0
    for name, pieces in (
        ("skip", [(skip_hbm.at[i], skip.at[i]) for i in range(8)]),
        ("grad", [(grad_hbm.at[i], gpad.at[1 + i, 1:5]) for i in range(8)]),
        ("win", [(win_hbm, win)]),
        ("sw", [(sw_hbm.at[m, h], sw.at[m, h]) for m in range(4) for h in cut_rows(sw, 4)]),
        ("wout", [(wout_hbm, wout)]),
        ("tw", [(tw_hbm.at[m, h], tw.at[m, h]) for m in range(4) for h in cut_rows(tw, 4)]),
        ("wup", [(wup_hbm.at[m], wup.at[m]) for m in range(9)]),
    ):
        loads[name] = Loads(
            [pltpu.make_async_copy(src, dst, load_sem.at[load_at + n])
             for n, (src, dst) in enumerate(pieces)]
        )
        load_at += len(pieces)
    for name in ("skip", "grad", "win", "sw"):
        loads[name].start()

    around = [(dr, dc) for dr in (-1, 0, 1) for dc in (-1, 0, 1) if (dr, dc) != (0, 0)]

    def beside(dr, dc):
        return {"row": (r + dr + N) % N, "col": (c + dc + N) % N}

    barrier = pltpu.get_barrier_semaphore()
    for d in range(1, N):
        pl.semaphore_signal(barrier, 1, device_id={"row": (r + d) % N}, device_id_type=MESH)
        pl.semaphore_signal(barrier, 1, device_id={"col": (c + d) % N}, device_id_type=MESH)
    for dr, dc in around:
        if dr != 0 and dc != 0:
            pl.semaphore_signal(barrier, 1, device_id=beside(dr, dc), device_id_type=MESH)
    x, y, z = r // 2, (c // 4) * 2 + r % 2, c % 4
    pl.semaphore_signal(
        barrier, 1, device_id={"row": x * 2 + (r + 1) % 2, "col": (c + 4) % N}, device_id_type=MESH
    )
    pl.semaphore_signal(barrier, 1, device_id={"grp": 1 - g}, device_id_type=MESH)
    pl.semaphore_wait(barrier, 2 * (N - 1) + 6)
    first = Sum(
        (x, y, z), g, SIZES1, x1, s1, z1, p1, t1, w1, v1, a1, fin1, ring_sem1, pair_sem1
    )
    second = Sum(
        (x, y, z), g, SIZES2, x2, s2, z2, p2, t2, w2, v2, a2, fin2, ring_sem2, pair_sem2
    )

    def send(stage, src, dst, axis, me):
        dst[me] = src[me]

        def step(d, carry):
            peer = (me + d) % N
            pltpu.make_async_remote_copy(
                src.at[peer], dst.at[me], swap_sem.at[stage, 0, peer], swap_sem.at[stage, 1, me],
                device_id={axis: peer}, device_id_type=MESH,
            ).start()
            return carry

        lax.fori_loop(1, N, step, 0)

    def arrive(stage, src, dst, axis, me):
        def step(d, carry):
            peer = (me + d) % N
            pltpu.make_async_remote_copy(
                src.at[peer], dst.at[peer], swap_sem.at[stage, 0, peer], swap_sem.at[stage, 1, peer],
                device_id={axis: peer}, device_id_type=MESH,
            ).wait()
            return carry

        lax.fori_loop(1, N, step, 0)

    def turn(src, dst, back):
        width = src.shape[2]
        rows = src[...].reshape(128, width)
        dst[...] = dot(permutation(back), rows).astype(BF).reshape(N, 16, width)

    def halo(k):
        dr, dc = around[k]
        src = gpad.at[
            {-1: pl.ds(1, 1), 0: pl.ds(1, 8), 1: pl.ds(8, 1)}[dr],
            {-1: pl.ds(1, 1), 0: pl.ds(1, 4), 1: pl.ds(4, 1)}[dc],
        ]
        dst = gpad.at[
            {-1: pl.ds(9, 1), 0: pl.ds(1, 8), 1: pl.ds(0, 1)}[dr],
            {-1: pl.ds(5, 1), 0: pl.ds(1, 4), 1: pl.ds(0, 1)}[dc],
        ]
        return pltpu.make_async_remote_copy(
            src, dst, halo_sem.at[0, k], halo_sem.at[1, k],
            device_id=beside(dr, dc), device_id_type=MESH,
        )

    loads["skip"].wait()
    means = []
    for p in range(2):
        total = jnp.zeros(skip.shape[2:], F32)
        for i in range(POOL):
            for j in range(POOL):
                total = total + skip[p * POOL + i, j].astype(F32)
        means.append(total * (1.0 / (POOL * POOL)))
    for f in range(N):
        rows = jnp.concatenate([means[0][8 * f:8 * f + 8], means[1][8 * f:8 * f + 8]], axis=0)
        a1s[f] = rows.astype(BF)
    pooled_t[...] = a1s[...].reshape(128, -1)
    send(0, a1s, a1r, "row", r)
    loads["grad"].wait()
    for k in range(8):
        halo(k).start()
    for name in ("wout", "tw", "wup"):
        loads[name].start()
    x1[660:] = jnp.zeros((12,) + x1.shape[1:], BF)
    x2[200:] = jnp.zeros((24,) + x2.shape[1:], BF)
    loads["win"].wait()
    coarse_t[...] = dot(pooled_t[...], win[...]).astype(BF)
    chan = gpad.shape[3]
    gexp[...] = jnp.zeros_like(gexp)

    def back_rows(first, last):
        def step(i, carry):
            total = jnp.zeros((256, chan), F32)
            for dy in range(3):
                for dx in range(3):
                    rows = gpad[i + 2 - dy, pl.ds(2 - dx, 4)].reshape(256, chan)
                    total = total + dot_nt(rows, wup[3 * dy + dx])
            low = total.astype(BF)
            gunited[i] = low.reshape(4, 64, chan)
            gexp[i // POOL] += jnp.sum(low.astype(F32).reshape(4, 64, chan), axis=0)
            return carry

        lax.fori_loop(first, last, step, 0)

    arrive(0, a1s, a1r, "row", r)
    turn(a1r, a2s, False)
    send(1, a2s, a2r, "col", c)
    arrive(1, a2s, a2r, "col", c)
    pooled_f[...] = a2r[...].reshape(128, chan)

    coarse_f[...] = dot(pooled_f[...], win[...]).astype(BF)
    loads["sw"].wait()
    for m, ref in enumerate((qs, ks, vs)):
        ref[...] = dot(coarse_f[...], sw[m]).astype(BF)
    attend(qs, ks, vs, probs_s, mix, None)
    b1s[...] = mix[...].reshape(b1s.shape)
    send(2, b1s, b1r, "col", c)
    loads["wup"].wait()
    for k in range(8):
        halo(k).wait()

    @pl.when(r == 0)
    def _():
        gpad[0] = jnp.zeros(gpad.shape[1:], BF)

    @pl.when(r == N - 1)
    def _():
        gpad[9] = jnp.zeros(gpad.shape[1:], BF)

    @pl.when(c == 0)
    def _():
        gpad[:, 0] = jnp.zeros((10,) + gpad.shape[2:], BF)

    @pl.when(c == N - 1)
    def _():
        gpad[:, 5] = jnp.zeros((10,) + gpad.shape[2:], BF)

    back_rows(0, 4)
    arrive(2, b1s, b1r, "col", c)
    turn(b1r, b2s, True)
    send(3, b2s, b2r, "row", r)
    loads["wout"].wait()
    loads["tw"].wait()
    back_rows(4, 8)
    for f in range(N):
        rows = jnp.concatenate([gexp[0, 8 * f:8 * f + 8], gexp[1, 8 * f:8 * f + 8]], axis=0)
        gexp_t[16 * f:16 * f + 16] = rows.astype(BF)
    gtimed[...] = dot(gexp_t[...], wout[...]).astype(BF)
    gmix[...] = dot(gtimed[...], tw[3]).astype(BF)
    arrive(3, b2s, b2r, "row", r)
    mix_t[...] = b2r[...].reshape(mix_t.shape)

    wide_nt(coarse_t, [(mix_t, sw, 3)], attended)
    for m, ref in enumerate((qt, kt, vt)):
        ref[...] = dot(attended[...], tw[m]).astype(BF)
    row_pixel = lax.broadcasted_iota(jnp.int32, (256, 128), 0) % 16 // 8
    key_pixel = lax.broadcasted_iota(jnp.int32, (256, 128), 1) % 16 // 8
    attend(qt, kt, vt, probs_t, mix, row_pixel == key_pixel)
    attend_back(qt, kt, vt, probs_t, gmix, gq, gk, gv)
    wide_nt(gtimed, [(gq, tw, 0), (gk, tw, 1), (gv, tw, 2)], gatt)
    c1s[...] = gatt[...].reshape(c1s.shape)
    send(4, c1s, c1r, "row", r)

    wide_nt(attended, [(mix, tw, 3)], timed)
    wide_tn(gexp_t, timed, x1, 23)
    expanded = dot_nt(timed[...], wout[...])
    for p in range(2):
        rows = jnp.concatenate(
            [expanded[16 * f + 8 * p:16 * f + 8 * p + 8] for f in range(N)], axis=0
        )

        def unite(i, carry):
            united = (skip[i].astype(F32) + rows[None]).astype(BF).reshape(256, chan)
            unit_t[:, pl.ds(pl.multiple_of(i * 256, 256), 256)] = united.T
            return carry

        lax.fori_loop(p * POOL, p * POOL + POOL, unite, 0)
    arrive(4, c1s, c1r, "row", r)
    turn(c1r, c2s, False)
    send(5, c2s, c2r, "col", c)

    def tap_rows(tap, cols):
        dy, dx = tap // 3, tap % 3
        return gpad[pl.ds(2 - dy, 8), pl.ds(2 - dx, 4), :, cols].reshape(2048, -1)

    def tap_step(tap, carry):
        put(x1, 2 * tap, dot(unit_t[...], tap_rows(tap, slice(0, 256))))
        return carry

    lax.fori_loop(0, 9, tap_step, 0)
    for taps, at in (((0, 1, 2, 3), 18), ((4, 5, 6, 7), 20)):
        rows = jnp.concatenate([tap_rows(tap, slice(256, chan)) for tap in taps], axis=1)
        put(x1, at, dot(unit_t[...], rows))
    rows = jnp.concatenate([tap_rows(8, slice(256, chan))] * 2, axis=1)
    put(x1, 22, dot(unit_t[...], rows))
    first.pair_send()
    arrive(5, c2s, c2r, "col", c)
    gatt[...] = c2r[...].reshape(gatt.shape)

    gmix[...] = dot(gatt[...], sw[3]).astype(BF)
    first.pair_add()
    first.spread_send(0)
    attend_back(qs, ks, vs, probs_s, gmix, gq, gk, gv)
    first.spread_add(0)
    first.spread_send(1)
    wide_nt(gatt, [(gq, sw, 0), (gk, sw, 1), (gv, sw, 2)], gcoarse)
    d1s[...] = dot_nt(gcoarse[...], win[...]).astype(BF).reshape(d1s.shape)
    send(6, d1s, d1r, "col", c)
    first.spread_add(1)
    first.last_send()
    wide_tn(pooled_f, gcoarse, x2, 0)
    second.pair_send()
    arrive(6, d1s, d1r, "col", c)
    turn(d1r, d2s, True)
    send(7, d2s, d2r, "row", r)
    first.last_add()
    first.gather_send(1)
    second.pair_add()
    second.spread_send(0)
    first.gather_wait(1)
    first.gather_send(0)
    arrive(7, d2s, d2r, "row", r)
    spread = d2r[...].reshape(128, chan).astype(F32) * (1.0 / (POOL * POOL))
    for p in range(2):
        rows = jnp.concatenate(
            [spread[16 * f + 8 * p:16 * f + 8 * p + 8] for f in range(N)], axis=0
        )

        def finish(i, carry):
            out[i] = (gunited[i].astype(F32) + rows[None]).astype(BF)
            return carry

        lax.fori_loop(p * POOL, p * POOL + POOL, finish, 0)
    second.spread_add(0)
    second.spread_send(1)
    first.gather_wait(0)
    second.spread_add(1)
    second.last_send()
    second.last_add()
    second.gather_send(1)
    second.gather_wait(1)
    second.gather_send(0)
    second.gather_wait(0)
    first.pair_done()

    def group_of(fin, at):
        return fin[pl.ds(20 * at, 20)].reshape(chan, 128)

    def whole(at, carry):
        up_out[at // 2, :, lanes(at % 2)] = group_of(fin1, at)
        return carry

    lax.fori_loop(0, 18, whole, 0)
    for at in range(5):
        rest = group_of(fin1, 18 + at)
        up_out[2 * at, :, 256:chan] = rest[:, :chan - 256]
        if at < 4:
            up_out[2 * at + 1, :, 256:chan] = rest[:, chan - 256:]

    def wide_group(at, carry):
        wide_out[0, :, lanes(at)] = group_of(fin1, 23 + at)
        return carry

    lax.fori_loop(0, 10, wide_group, 0)
    second.pair_done()

    def wide_group2(at, carry):
        wide_out[1, :, lanes(at)] = group_of(fin2, at)
        return carry

    lax.fori_loop(0, 10, wide_group2, 0)


def shards(skip, w_up, w_in, w_out, spatial_w, temporal_w, grad_out):
    frames, tile_h, tile_w, chan = skip.shape
    wide = w_in.shape[1]
    att = spatial_w.shape[2]
    skip_t = jnp.transpose(skip, (1, 2, 0, 3))
    grad_t = jnp.transpose(grad_out, (1, 2, 0, 3))
    w_out_t = w_out.T

    def vm(shape, dtype=BF):
        return pltpu.VMEM(shape, dtype)

    tok = 128
    swaps = []
    for width in (chan, att, wide, chan):
        swaps += [vm((N, 16, width))] * 4

    def sums(sizes):
        u = sum(sizes)
        return [vm((n * u, 16, 128)) for n in (32, 16, 16, 4, 4, 1, 4, 4, 32)]

    scratch = [
        vm(skip_t.shape), vm((tile_h + 2, tile_w + 2, frames, chan)), vm(w_up.shape),
        vm(w_in.shape), vm(w_out_t.shape), vm(spatial_w.shape), vm(temporal_w.shape),
        *swaps,
        vm((tok, chan)), vm((tok, wide)), vm((tok, chan)), vm((tok, wide)),
        vm(skip_t.shape), vm((2, frames, chan), F32), vm((tok, chan)), vm((tok, wide)),
        vm((tok, wide)),
        vm((tok, att)), vm((tok, att)), vm((tok, att)), vm((att // 128, 256, 128), F32),
        vm((tok, att)), vm((tok, att)), vm((tok, att)), vm((att // 128, 256, 128), F32),
        vm((tok, att)), vm((tok, att)), vm((tok, wide)), vm((tok, wide)),
        vm((tok, att)), vm((tok, att)), vm((tok, att)), vm((tok, att)), vm((tok, wide)),
        vm((chan, frames * tile_h * tile_w)),
        *sums(SIZES1), *sums(SIZES2),
        pltpu.SemaphoreType.DMA((59,)), pltpu.SemaphoreType.DMA((2, 8)),
        pltpu.SemaphoreType.DMA((8, 2, N)),
        *[pltpu.SemaphoreType.DMA((5, 2, 3, 4)), pltpu.SemaphoreType.DMA((2, 2, 12))] * 2,
    ]
    grad_skip, up, wide_grads = pl.pallas_call(
        main_kernel,
        out_shape=(
            jax.ShapeDtypeStruct(skip_t.shape, BF),
            jax.ShapeDtypeStruct(w_up.shape, BF),
            jax.ShapeDtypeStruct((2,) + w_in.shape, BF),
        ),
        in_specs=[pl.BlockSpec(memory_space=pl.ANY)] * 7,
        out_specs=[pl.BlockSpec(memory_space=pltpu.VMEM)] * 3,
        scratch_shapes=scratch,
        compiler_params=pltpu.CompilerParams(
            collective_id=0, has_side_effects=True, vmem_limit_bytes=60 * 1024 * 1024
        ),
        name="backward",
    )(skip_t, grad_t, w_up, w_in, w_out_t, spatial_w, temporal_w)
    grad_w_out, grad_w_in = wide_grads[0].astype(F32).T, wide_grads[1].astype(F32)
    return (jnp.transpose(grad_skip, (2, 0, 1, 3)), up.astype(F32), grad_w_in, grad_w_out)


def solution(mesh):
    in_specs = (P("grp", "row", "col", None), P(), P(), P(), P(), P(), P("grp", "row", "col", None))
    out_specs = (P("grp", "row", "col", None), P(), P(), P())
    return jax.shard_map(shards, mesh=mesh, in_specs=in_specs, out_specs=out_specs, check_vma=False)
```

```python
import jax
import jax.numpy as jnp
from jax import lax
from jax.experimental import pallas as pl
from jax.experimental.pallas import tpu as pltpu
from jax.sharding import PartitionSpec as P

HD = 64
POOL = 4
N = 8
F32 = jnp.float32
BF = jnp.bfloat16
MESH = pl.DeviceIdType.MESH
SIZES1 = (7, 7, 7)
SIZES2 = (3, 2, 2)


def dot(a, b):
    return lax.dot_general(a, b, (((1,), (0,)), ((), ())), preferred_element_type=F32)


def dot_nt(a, b):
    return lax.dot_general(a, b, (((1,), (1,)), ((), ())), preferred_element_type=F32)


def dot_tn(a, b):
    return lax.dot_general(a, b, (((0,), (0,)), ((), ())), preferred_element_type=F32)


def permutation(back):
    to = lax.broadcasted_iota(jnp.int32, (128, 128), 1 if back else 0)
    fro = lax.broadcasted_iota(jnp.int32, (128, 128), 0 if back else 1)
    wanted = (to % 16 // 2) * 16 + (to % 2) * 8 + to // 16
    return jnp.where(fro == wanted, 1.0, 0.0).astype(BF)


def halves():
    lane = lax.broadcasted_iota(jnp.int32, (128, 128), 1)
    low = jnp.where(lane < HD, 1.0, 0.0)
    return low.astype(BF), (1.0 - low).astype(BF), lane < HD


def lanes(pair):
    return pl.ds(pl.multiple_of(pair * 128, 128), 128)


def attend(q, k, v, probs, mixed, same_set):
    low, high, is_low = halves()

    def pair_step(pair, carry):
        cols = lanes(pair)
        q2, k2, v2 = q[:, cols], k[:, cols], v[:, cols]
        stacked = jnp.concatenate([q2 * low, q2 * high], axis=0)
        scores = dot_nt(stacked, k2) * (HD ** -0.5)
        if same_set is not None:
            scores = jnp.where(same_set, scores, -3e38)
        shifted = jnp.exp(scores - jnp.max(scores, axis=-1, keepdims=True))
        prob = shifted / jnp.sum(shifted, axis=-1, keepdims=True)
        probs[pair] = prob
        out = dot(prob.astype(BF), v2)
        mixed[:, cols] = jnp.where(is_low, out[:128], out[128:]).astype(BF)
        return carry

    lax.fori_loop(0, q.shape[1] // 128, pair_step, 0)


def attend_back(q, k, v, probs, gmix, gq, gk, gv):
    low, high, is_low = halves()

    def pair_step(pair, carry):
        cols = lanes(pair)
        q2, k2, v2, g2 = q[:, cols], k[:, cols], v[:, cols], gmix[:, cols]
        stacked = jnp.concatenate([q2 * low, q2 * high], axis=0)
        gstacked = jnp.concatenate([g2 * low, g2 * high], axis=0)
        prob = probs[pair]
        gprob = dot_nt(gstacked, v2)
        inner = jnp.sum(gprob * prob, axis=-1, keepdims=True)
        gscore = prob * (gprob - inner) * (HD ** -0.5)
        gv[:, cols] = dot_tn(prob.astype(BF), gstacked).astype(BF)
        gscore = gscore.astype(BF)
        out = dot(gscore, k2)
        gq[:, cols] = jnp.where(is_low, out[:128], out[128:]).astype(BF)
        gk[:, cols] = dot_tn(gscore, stacked).astype(BF)
        return carry

    lax.fori_loop(0, q.shape[1] // 128, pair_step, 0)


def wide_nt(base, pairs, out):
    def step(at, carry):
        cols = pl.ds(pl.multiple_of(at * 256, 256), 256)
        total = base[:, cols].astype(F32)
        for x, matrix, index in pairs:
            total = total + dot_nt(x[...], matrix[index, cols, :])
        out[:, cols] = total.astype(BF)
        return carry

    lax.fori_loop(0, out.shape[1] // 256, step, 0)


def put(units, group, product):
    for n in range(product.shape[1] // 128):
        part = product[:, 128 * n:128 * n + 128].astype(BF).reshape(-1, 16, 128)
        size = part.shape[0]
        units[pl.ds((group + n) * size, size)] = part


def wide_tn(left, right, units, group):
    def step(at, carry):
        cols = pl.ds(pl.multiple_of(at * 256, 256), 256)
        put(units, group + 2 * at, dot_tn(left[...], right[:, cols]))
        return carry

    lax.fori_loop(0, right.shape[1] // 256, step, 0)


class Sum:
    def __init__(self, place, g, sizes, blocks, paired, slots, part, slots2, own, slots3, row, fin,
                 ring, pair):
        self.place, self.g, self.sizes = place, g, sizes
        self.blocks, self.paired, self.slots, self.part = blocks, paired, slots, part
        self.slots2, self.own, self.slots3, self.row, self.fin = slots2, own, slots3, row, fin
        self.ring, self.pair = ring, pair
        self.offs = [sum(sizes[:k]) for k in range(3)]
        self.total = 16 * sum(sizes)

    def big(self, k, at, base=0):
        return pl.ds(base + 16 * self.offs[k] + at * (4 * self.sizes[k]), 4 * self.sizes[k])

    def small(self, k, at):
        return pl.ds(4 * self.offs[k] + at * self.sizes[k], self.sizes[k])

    def line(self, k):
        return pl.ds(4 * self.offs[k], 4 * self.sizes[k])

    def mine(self, k):
        return pl.ds(self.offs[k], self.sizes[k])

    def me(self, k, stage):
        return self.place[(k + stage) % 3]

    def peer(self, k, stage, at):
        x, y, z = self.place
        axis = (k + stage) % 3
        if axis == 0:
            return {"row": at * 2 + y % 2}
        if axis == 1:
            return {"row": x * 2 + at % 2, "col": (at // 2) * 4 + z}
        return {"col": (y // 2) * 4 + at}

    def copy(self, src, dst, sem, k, stage, slot_s, slot_r, at):
        return pltpu.make_async_remote_copy(
            src, dst, self.ring.at[sem, 0, k, slot_s], self.ring.at[sem, 1, k, slot_r],
            device_id=self.peer(k, stage, at), device_id_type=MESH,
        )

    def others(self, stage, step):
        for k in range(3):
            me = self.me(k, stage)

            def one(d, carry):
                step(k, me, (me + d) % 4)
                return carry

            lax.fori_loop(1, 4, one, 0)

    def quarters(self, step):
        for k in range(3):
            def one(at, carry):
                step(k, at)
                return carry

            lax.fori_loop(0, 4, one, 0)

    def pair_copy(self, k, at):
        return pltpu.make_async_remote_copy(
            self.blocks.at[self.big(k, at, (1 - self.g) * self.total)],
            self.paired.at[self.big(k, at)],
            self.pair.at[0, 0, 4 * k + at], self.pair.at[0, 1, 4 * k + at],
            device_id={"grp": 1 - self.g}, device_id_type=MESH,
        )

    def pair_send(self):
        self.quarters(lambda k, at: self.pair_copy(k, at).start())

    def pair_add(self):
        def step(k, at):
            self.pair_copy(k, at).wait()
            some = self.big(k, at)
            total = self.blocks[self.big(k, at, self.g * self.total)].astype(F32)
            self.paired[some] = (total + self.paired[some].astype(F32)).astype(BF)

        self.quarters(step)

    def spread_copy(self, stage, k, me, at, arriving):
        slot = at if arriving else me
        if stage == 0:
            src, dst = self.paired.at[self.big(k, at)], self.slots.at[self.big(k, slot)]
        else:
            src, dst = self.part.at[self.small(k, at)], self.slots2.at[self.small(k, slot)]
        return self.copy(src, dst, stage, k, stage, at, slot, at)

    def spread_send(self, stage):
        self.others(
            stage, lambda k, me, at: self.spread_copy(stage, k, me, at, False).start()
        )

    def spread_add(self, stage):
        for k in range(3):
            me = self.me(k, stage)

            def one(d, carry):
                self.spread_copy(stage, k, me, (me + d) % 4, True).wait()
                return carry

            lax.fori_loop(1, 4, one, 0)
            if stage == 0:
                total = self.paired[self.big(k, me)].astype(F32)
                for d in range(1, 4):
                    total = total + self.slots[self.big(k, (me + d) % 4)].astype(F32)
                self.part[self.line(k)] = total.astype(BF)
            else:
                total = self.part[self.small(k, me)].astype(F32)
                for d in range(1, 4):
                    total = total + self.slots2[self.small(k, (me + d) % 4)].astype(F32)
                self.own[self.mine(k)] = total.astype(BF)

    def last_copy(self, k, me, at, arriving):
        slot = at if arriving else me
        dst = self.slots3.at[self.small(k, slot)]
        return self.copy(self.own.at[self.mine(k)], dst, 2, k, 2, at, slot, at)

    def last_send(self):
        self.others(2, lambda k, me, at: self.last_copy(k, me, at, False).start())

    def last_add(self):
        self.others(2, lambda k, me, at: self.last_copy(k, me, at, True).wait())
        for k in range(3):
            self.slots3[self.small(k, self.me(k, 2))] = self.own[self.mine(k)]
            total = self.slots3[self.small(k, 0)].astype(F32)
            for at in range(1, 4):
                total = total + self.slots3[self.small(k, at)].astype(F32)
            self.row[self.small(k, self.me(k, 1))] = total.astype(BF)

    def gather_copy(self, stage, k, me, at, arriving):
        slot = at if arriving else me
        if stage == 1:
            src, dst = self.row.at[self.small(k, me)], self.row.at[self.small(k, slot)]
        else:
            src = self.row.at[self.line(k)]
            dst = self.fin.at[self.big(k, slot, self.g * self.total)]
        return self.copy(src, dst, 4 - stage, k, stage, at, slot, at)

    def gather_send(self, stage):
        self.others(
            stage, lambda k, me, at: self.gather_copy(stage, k, me, at, False).start()
        )
        if stage == 0:
            for k in range(3):
                me = self.me(k, 0)
                self.fin[self.big(k, me, self.g * self.total)] = self.row[self.line(k)]
                self.over(k, me, True).start()

    def gather_wait(self, stage):
        def step(k, me, at):
            self.gather_copy(stage, k, me, at, True).wait()
            if stage == 0:
                self.over(k, at, True).start()

        self.others(stage, step)

    def over(self, k, at, mine):
        half = self.g if mine else 1 - self.g
        part = self.fin.at[self.big(k, at, half * self.total)]
        return pltpu.make_async_remote_copy(
            part, part, self.pair.at[1, 0, 4 * k + at], self.pair.at[1, 1, 4 * k + at],
            device_id={"grp": 1 - self.g}, device_id_type=MESH,
        )

    def pair_done(self):
        def step(k, at):
            self.over(k, at, True).wait_send()
            self.over(k, at, False).wait_recv()

        self.quarters(step)


class Loads:
    def __init__(self, copies):
        self.copies = copies

    def start(self):
        for copy in self.copies:
            copy.start()

    def wait(self):
        for copy in self.copies:
            copy.wait()


def cut_rows(ref, count):
    size = ref.shape[1] // count
    return [pl.ds(size * n, size) for n in range(count)]


def main_kernel(
    skip_hbm, grad_hbm, wup_hbm, win_hbm, wout_hbm, sw_hbm, tw_hbm,
    out, up_out, wide_out,
    skip, gpad, wup, win, wout, sw, tw,
    a1s, a1r, a2s, a2r, b1s, b1r, b2s, b2r, c1s, c1r, c2s, c2r, d1s, d1r, d2s, d2r,
    pooled_t, coarse_t, pooled_f, coarse_f, gunited, gexp, gexp_t, gtimed, gcoarse,
    qs, ks, vs, probs_s, qt, kt, vt, probs_t, mix, mix_t, attended, timed, gmix, gq, gk, gv, gatt,
    unit_t, skip_raw, grad_raw,
    x1, s1, z1, p1, t1, w1, v1, a1, fin1, x2, s2, z2, p2, t2, w2, v2, a2, fin2,
    load_sem, halo_sem, swap_sem, ring_sem1, pair_sem1, ring_sem2, pair_sem2,
):
    r, c, g = lax.axis_index("row"), lax.axis_index("col"), lax.axis_index("grp")
    frame_cuts = [pl.ds(8 * n, 8) for n in range(8)]
    loads = {}
    load_at = 0
    for name, pieces in (
        ("skip", [(skip_hbm.at[h], skip_raw.at[h]) for h in frame_cuts]),
        ("grad", [(grad_hbm.at[h], grad_raw.at[h]) for h in frame_cuts]),
        ("win", [(win_hbm, win)]),
        ("sw", [(sw_hbm.at[m, h], sw.at[m, h]) for m in range(4) for h in cut_rows(sw, 4)]),
        ("wout", [(wout_hbm, wout)]),
        ("tw", [(tw_hbm.at[m, h], tw.at[m, h]) for m in range(4) for h in cut_rows(tw, 4)]),
        ("wup", [(wup_hbm.at[m], wup.at[m]) for m in range(9)]),
    ):
        loads[name] = Loads(
            [pltpu.make_async_copy(src, dst, load_sem.at[load_at + n])
             for n, (src, dst) in enumerate(pieces)]
        )
        load_at += len(pieces)
    for name in ("skip", "grad", "win", "wup", "sw", "wout", "tw"):
        loads[name].start()

    around = [(dr, dc) for dr in (-1, 0, 1) for dc in (-1, 0, 1) if (dr, dc) != (0, 0)]

    def beside(dr, dc):
        return {"row": (r + dr + N) % N, "col": (c + dc + N) % N}

    barrier = pltpu.get_barrier_semaphore()
    for d in range(1, N):
        pl.semaphore_signal(barrier, 1, device_id={"row": (r + d) % N}, device_id_type=MESH)
        pl.semaphore_signal(barrier, 1, device_id={"col": (c + d) % N}, device_id_type=MESH)
    for dr, dc in around:
        if dr != 0 and dc != 0:
            pl.semaphore_signal(barrier, 1, device_id=beside(dr, dc), device_id_type=MESH)
    x, y, z = r // 2, (c // 4) * 2 + r % 2, c % 4
    pl.semaphore_signal(
        barrier, 1, device_id={"row": x * 2 + (r + 1) % 2, "col": (c + 4) % N}, device_id_type=MESH
    )
    pl.semaphore_signal(barrier, 1, device_id={"grp": 1 - g}, device_id_type=MESH)
    first = Sum(
        (x, y, z), g, SIZES1, x1, s1, z1, p1, t1, w1, v1, a1, fin1, ring_sem1, pair_sem1
    )
    second = Sum(
        (x, y, z), g, SIZES2, x2, s2, z2, p2, t2, w2, v2, a2, fin2, ring_sem2, pair_sem2
    )

    def send(stage, src, dst, axis, me):
        dst[me] = src[me]

        def step(d, carry):
            peer = (me + d) % N
            pltpu.make_async_remote_copy(
                src.at[peer], dst.at[me], swap_sem.at[stage, 0, peer], swap_sem.at[stage, 1, me],
                device_id={axis: peer}, device_id_type=MESH,
            ).start()
            return carry

        lax.fori_loop(1, N, step, 0)

    def arrive(stage, src, dst, axis, me):
        def step(d, carry):
            peer = (me + d) % N
            pltpu.make_async_remote_copy(
                src.at[peer], dst.at[peer], swap_sem.at[stage, 0, peer], swap_sem.at[stage, 1, peer],
                device_id={axis: peer}, device_id_type=MESH,
            ).wait()
            return carry

        lax.fori_loop(1, N, step, 0)

    def turn(src, dst, back):
        width = src.shape[2]
        rows = src[...].reshape(128, width)
        dst[...] = dot(permutation(back), rows).astype(BF).reshape(N, 16, width)

    def halo(k):
        dr, dc = around[k]
        src = gpad.at[
            {-1: pl.ds(1, 1), 0: pl.ds(1, 8), 1: pl.ds(8, 1)}[dr],
            {-1: pl.ds(1, 1), 0: pl.ds(1, 4), 1: pl.ds(4, 1)}[dc],
        ]
        dst = gpad.at[
            {-1: pl.ds(9, 1), 0: pl.ds(1, 8), 1: pl.ds(0, 1)}[dr],
            {-1: pl.ds(5, 1), 0: pl.ds(1, 4), 1: pl.ds(0, 1)}[dc],
        ]
        return pltpu.make_async_remote_copy(
            src, dst, halo_sem.at[0, k], halo_sem.at[1, k],
            device_id=beside(dr, dc), device_id_type=MESH,
        )

    def halo_each(k, way, act):
        tests = [
            {-1: at > 0, 1: at < N - 1}[way * d]
            for at, d in zip((r, c), around[k]) if d != 0
        ]

        @pl.when(tests[0] if len(tests) == 1 else jnp.logical_and(*tests))
        def _():
            act(halo(k))

    loads["skip"].wait()
    for i in range(8):
        skip[i] = jnp.swapaxes(skip_raw[:, i], 0, 1)
    means = []
    for p in range(2):
        total = jnp.zeros(skip.shape[2:], F32)
        for i in range(POOL):
            for j in range(POOL):
                total = total + skip[p * POOL + i, j].astype(F32)
        means.append(total * (1.0 / (POOL * POOL)))
    for f in range(N):
        rows = jnp.concatenate([means[0][8 * f:8 * f + 8], means[1][8 * f:8 * f + 8]], axis=0)
        a1s[f] = rows.astype(BF)
    pooled_t[...] = a1s[...].reshape(128, -1)
    loads["grad"].wait()
    for i in range(8):
        gpad[1 + i, 1:5] = jnp.swapaxes(grad_raw[:, i], 0, 1)
    pl.semaphore_wait(barrier, 2 * (N - 1) + 6)
    send(0, a1s, a1r, "row", r)
    x1[660:] = jnp.zeros((12,) + x1.shape[1:], BF)
    x2[200:] = jnp.zeros((24,) + x2.shape[1:], BF)
    loads["win"].wait()
    coarse_t[...] = dot(pooled_t[...], win[...]).astype(BF)
    chan = gpad.shape[3]
    def tap_rows(tap, cols):
        dy, dx = tap // 3, tap % 3
        return gpad[pl.ds(2 - dy, 8), pl.ds(2 - dx, 4), :, cols].reshape(2048, -1)

    def tap_step(tap, carry):
        put(x1, 2 * tap, dot(unit_t[...], tap_rows(tap, slice(0, 256))))
        return carry

    def weight_taps(first_tap, last_tap):
        lax.fori_loop(first_tap, last_tap, tap_step, 0)

    def back_taps(rows_of, size):
        total = jnp.zeros((size, chan), F32)
        for dy in range(3):
            for dx in range(3):
                total = total + dot_nt(rows_of(dy, dx).reshape(size, chan), wup[3 * dy + dx])
        return total.astype(BF)

    def back_inner(p):
        low = back_taps(lambda dy, dx: gpad[3 * p + 3 - dy:3 * p + 6 - dy, 3 - dx:5 - dx], 384)
        low = low.reshape(3, 2, 64, chan)
        gunited[3 * p + 1:3 * p + 4, 1:3] = low
        gexp[p] = jnp.sum(low.astype(F32), axis=(0, 1))

    def back_sides(p, carry):
        def rows_of(dy, dx):
            near = pl.ds(3 * p + 3 - dy, 3)
            return jnp.concatenate([gpad[near, 2 - dx], gpad[near, 5 - dx]], axis=0)

        low = back_taps(rows_of, 384).reshape(2, 3, 64, chan)
        gunited[pl.ds(3 * p + 1, 3), 0] = low[0]
        gunited[pl.ds(3 * p + 1, 3), 3] = low[1]
        gexp[p] += jnp.sum(low.astype(F32), axis=(0, 1))
        return carry

    def back_ends(p, carry):
        low = back_taps(lambda dy, dx: gpad[7 * p + 2 - dy, 2 - dx:6 - dx], 256)
        low = low.reshape(4, 64, chan)
        gunited[7 * p] = low
        gexp[p] += jnp.sum(low.astype(F32), axis=0)
        return carry

    loads["wup"].wait()
    back_inner(0)
    arrive(0, a1s, a1r, "row", r)
    turn(a1r, a2s, False)
    send(1, a2s, a2r, "col", c)
    back_inner(1)
    arrive(1, a2s, a2r, "col", c)
    for k in (3, 4):
        halo_each(k, 1, lambda copy: copy.start())
    pooled_f[...] = a2r[...].reshape(128, chan)

    coarse_f[...] = dot(pooled_f[...], win[...]).astype(BF)
    loads["sw"].wait()
    for m, ref in enumerate((qs, ks, vs)):
        ref[...] = dot(coarse_f[...], sw[m]).astype(BF)
    attend(qs, ks, vs, probs_s, mix, None)
    b1s[...] = mix[...].reshape(b1s.shape)
    send(2, b1s, b1r, "col", c)
    arrive(2, b1s, b1r, "col", c)
    turn(b1r, b2s, True)
    send(3, b2s, b2r, "row", r)
    for k in (1, 6, 0, 2, 5, 7):
        halo_each(k, 1, lambda copy: copy.start())
    arrive(3, b2s, b2r, "row", r)
    mix_t[...] = b2r[...].reshape(mix_t.shape)

    loads["wout"].wait()
    loads["tw"].wait()
    wide_nt(coarse_t, [(mix_t, sw, 3)], attended)
    for m, ref in enumerate((qt, kt, vt)):
        ref[...] = dot(attended[...], tw[m]).astype(BF)
    row_pixel = lax.broadcasted_iota(jnp.int32, (256, 128), 0) % 16 // 8
    key_pixel = lax.broadcasted_iota(jnp.int32, (256, 128), 1) % 16 // 8
    attend(qt, kt, vt, probs_t, mix, row_pixel == key_pixel)
    wide_nt(attended, [(mix, tw, 3)], timed)
    expanded = dot_nt(timed[...], wout[...])
    for p in range(2):
        rows = jnp.concatenate(
            [expanded[16 * f + 8 * p:16 * f + 8 * p + 8] for f in range(N)], axis=0
        )

        def unite(i, carry):
            united = (skip[i].astype(F32) + rows[None]).astype(BF).reshape(256, chan)
            unit_t[:, pl.ds(pl.multiple_of(i * 256, 256), 256)] = united.T
            return carry

        lax.fori_loop(p * POOL, p * POOL + POOL, unite, 0)
    for k in range(8):
        halo_each(k, 1, lambda copy: copy.wait_send())
        halo_each(k, -1, lambda copy: copy.wait_recv())

    @pl.when(r == 0)
    def _():
        gpad[0] = jnp.zeros(gpad.shape[1:], BF)

    @pl.when(r == N - 1)
    def _():
        gpad[9] = jnp.zeros(gpad.shape[1:], BF)

    @pl.when(c == 0)
    def _():
        gpad[:, 0] = jnp.zeros((10,) + gpad.shape[2:], BF)

    @pl.when(c == N - 1)
    def _():
        gpad[:, 5] = jnp.zeros((10,) + gpad.shape[2:], BF)

    lax.fori_loop(0, 2, back_sides, 0)
    lax.fori_loop(0, 2, back_ends, 0)
    for f in range(N):
        rows = jnp.concatenate([gexp[0, 8 * f:8 * f + 8], gexp[1, 8 * f:8 * f + 8]], axis=0)
        gexp_t[16 * f:16 * f + 16] = rows.astype(BF)
    gtimed[...] = dot(gexp_t[...], wout[...]).astype(BF)
    gmix[...] = dot(gtimed[...], tw[3]).astype(BF)
    attend_back(qt, kt, vt, probs_t, gmix, gq, gk, gv)
    wide_nt(gtimed, [(gq, tw, 0), (gk, tw, 1), (gv, tw, 2)], gatt)
    c1s[...] = gatt[...].reshape(c1s.shape)
    send(4, c1s, c1r, "row", r)

    wide_tn(gexp_t, timed, x1, 23)
    weight_taps(0, 5)
    arrive(4, c1s, c1r, "row", r)
    turn(c1r, c2s, False)
    send(5, c2s, c2r, "col", c)

    weight_taps(5, 9)
    for taps, at in (((0, 1, 2, 3), 18), ((4, 5, 6, 7), 20)):
        rows = jnp.concatenate([tap_rows(tap, slice(256, chan)) for tap in taps], axis=1)
        put(x1, at, dot(unit_t[...], rows))
    rows = jnp.concatenate([tap_rows(8, slice(256, chan))] * 2, axis=1)
    put(x1, 22, dot(unit_t[...], rows))
    first.pair_send()
    arrive(5, c2s, c2r, "col", c)
    gatt[...] = c2r[...].reshape(gatt.shape)

    gmix[...] = dot(gatt[...], sw[3]).astype(BF)
    first.pair_add()
    first.spread_send(0)
    attend_back(qs, ks, vs, probs_s, gmix, gq, gk, gv)
    wide_nt(gatt, [(gq, sw, 0), (gk, sw, 1), (gv, sw, 2)], gcoarse)
    d1s[...] = dot_nt(gcoarse[...], win[...]).astype(BF).reshape(d1s.shape)
    send(6, d1s, d1r, "col", c)
    wide_tn(pooled_f, gcoarse, x2, 0)
    second.pair_send()
    arrive(6, d1s, d1r, "col", c)
    turn(d1r, d2s, True)
    send(7, d2s, d2r, "row", r)
    first.spread_add(0)
    first.spread_send(1)
    second.pair_add()
    second.spread_send(0)
    arrive(7, d2s, d2r, "row", r)
    spread = d2r[...].reshape(128, chan).astype(F32) * (1.0 / (POOL * POOL))
    for p in range(2):
        rows = jnp.concatenate(
            [spread[16 * f + 8 * p:16 * f + 8 * p + 8] for f in range(N)], axis=0
        )

        def finish(i, carry):
            full = (gunited[i].astype(F32) + rows[None]).astype(BF)
            skip_raw[:, i] = jnp.swapaxes(full, 0, 1)
            return carry

        lax.fori_loop(p * POOL, p * POOL + POOL, finish, 0)
    stores = Loads([
        pltpu.make_async_copy(skip_raw.at[h], out.at[h], load_sem.at[n])
        for n, h in enumerate(frame_cuts)
    ])
    stores.start()
    first.spread_add(1)
    first.last_send()
    second.spread_add(0)
    second.spread_send(1)
    first.last_add()
    first.gather_send(1)
    second.spread_add(1)
    second.last_send()
    first.gather_wait(1)
    first.gather_send(0)
    second.last_add()
    second.gather_send(1)
    second.gather_wait(1)
    second.gather_send(0)
    first.gather_wait(0)
    second.gather_wait(0)
    first.pair_done()

    def group_of(fin, at):
        return fin[pl.ds(20 * at, 20)].reshape(chan, 128)

    def whole(at, carry):
        up_out[at // 2, :, lanes(at % 2)] = group_of(fin1, at)
        return carry

    lax.fori_loop(0, 18, whole, 0)
    for at in range(5):
        rest = group_of(fin1, 18 + at)
        up_out[2 * at, :, 256:chan] = rest[:, :chan - 256]
        if at < 4:
            up_out[2 * at + 1, :, 256:chan] = rest[:, chan - 256:]

    def wide_group(at, carry):
        wide_out[0, :, lanes(at)] = group_of(fin1, 23 + at)
        return carry

    lax.fori_loop(0, 10, wide_group, 0)
    second.pair_done()

    def wide_group2(at, carry):
        wide_out[1, :, lanes(at)] = group_of(fin2, at)
        return carry

    lax.fori_loop(0, 10, wide_group2, 0)
    stores.wait()


def shards(skip, w_up, w_in, w_out, spatial_w, temporal_w, grad_out):
    frames, tile_h, tile_w, chan = skip.shape
    wide = w_in.shape[1]
    att = spatial_w.shape[2]
    skip_shape = (tile_h, tile_w, frames, chan)
    w_out_t = w_out.T

    def vm(shape, dtype=BF):
        return pltpu.VMEM(shape, dtype)

    tok = 128
    swaps = []
    for width in (chan, att, wide, chan):
        swaps += [vm((N, 16, width))] * 4

    def sums(sizes):
        u = sum(sizes)
        return [vm((n * u, 16, 128)) for n in (32, 16, 16, 4, 4, 1, 4, 4, 32)]

    scratch = [
        vm(skip_shape), vm((tile_h + 2, tile_w + 2, frames, chan)), vm(w_up.shape),
        vm(w_in.shape), vm(w_out_t.shape), vm(spatial_w.shape), vm(temporal_w.shape),
        *swaps,
        vm((tok, chan)), vm((tok, wide)), vm((tok, chan)), vm((tok, wide)),
        vm(skip_shape), vm((2, frames, chan), F32), vm((tok, chan)), vm((tok, wide)),
        vm((tok, wide)),
        vm((tok, att)), vm((tok, att)), vm((tok, att)), vm((att // 128, 256, 128), F32),
        vm((tok, att)), vm((tok, att)), vm((tok, att)), vm((att // 128, 256, 128), F32),
        vm((tok, att)), vm((tok, att)), vm((tok, wide)), vm((tok, wide)),
        vm((tok, att)), vm((tok, att)), vm((tok, att)), vm((tok, att)), vm((tok, wide)),
        vm((chan, frames * tile_h * tile_w)),
        vm(skip.shape), vm(skip.shape),
        *sums(SIZES1), *sums(SIZES2),
        pltpu.SemaphoreType.DMA((59,)), pltpu.SemaphoreType.DMA((2, 8)),
        pltpu.SemaphoreType.DMA((8, 2, N)),
        *[pltpu.SemaphoreType.DMA((5, 2, 3, 4)), pltpu.SemaphoreType.DMA((2, 2, 12))] * 2,
    ]
    grad_skip, up, wide_grads = pl.pallas_call(
        main_kernel,
        out_shape=(
            jax.ShapeDtypeStruct(skip.shape, BF),
            jax.ShapeDtypeStruct(w_up.shape, BF),
            jax.ShapeDtypeStruct((2,) + w_in.shape, BF),
        ),
        in_specs=[pl.BlockSpec(memory_space=pl.ANY)] * 7,
        out_specs=[pl.BlockSpec(memory_space=pl.ANY)] + [pl.BlockSpec(memory_space=pltpu.VMEM)] * 2,
        scratch_shapes=scratch,
        compiler_params=pltpu.CompilerParams(
            collective_id=0, has_side_effects=True, vmem_limit_bytes=60 * 1024 * 1024
        ),
        name="backward",
    )(skip, grad_out, w_up, w_in, w_out_t, spatial_w, temporal_w)
    grad_w_out, grad_w_in = wide_grads[0].astype(F32).T, wide_grads[1].astype(F32)
    return (grad_skip, up.astype(F32), grad_w_in, grad_w_out)


def solution(mesh):
    in_specs = (P("grp", "row", "col", None), P(), P(), P(), P(), P(), P("grp", "row", "col", None))
    out_specs = (P("grp", "row", "col", None), P(), P(), P())
    return jax.shard_map(shards, mesh=mesh, in_specs=in_specs, out_specs=out_specs, check_vma=False)
```

```python
import jax
import jax.numpy as jnp
from jax import lax
from jax.experimental import pallas as pl
from jax.experimental.pallas import tpu as pltpu
from jax.sharding import PartitionSpec as P

HD = 64
POOL = 4
N = 8
F32 = jnp.float32
BF = jnp.bfloat16
MESH = pl.DeviceIdType.MESH
SIZES1 = (7, 7, 7)
SIZES2 = (3, 2, 2)


def dot(a, b):
    return lax.dot_general(a, b, (((1,), (0,)), ((), ())), preferred_element_type=F32)


def dot_nt(a, b):
    return lax.dot_general(a, b, (((1,), (1,)), ((), ())), preferred_element_type=F32)


def dot_tn(a, b):
    return lax.dot_general(a, b, (((0,), (0,)), ((), ())), preferred_element_type=F32)


def permutation(back):
    to = lax.broadcasted_iota(jnp.int32, (128, 128), 1 if back else 0)
    fro = lax.broadcasted_iota(jnp.int32, (128, 128), 0 if back else 1)
    wanted = (to % 16 // 2) * 16 + (to % 2) * 8 + to // 16
    return jnp.where(fro == wanted, 1.0, 0.0).astype(BF)


def halves():
    lane = lax.broadcasted_iota(jnp.int32, (128, 128), 1)
    low = jnp.where(lane < HD, 1.0, 0.0)
    return low.astype(BF), (1.0 - low).astype(BF), lane < HD


def lanes(pair):
    return pl.ds(pl.multiple_of(pair * 128, 128), 128)


def attend(q, k, v, probs, mixed, same_set):
    low, high, is_low = halves()

    def pair_step(pair, carry):
        cols = lanes(pair)
        q2, k2, v2 = q[:, cols], k[:, cols], v[:, cols]
        stacked = jnp.concatenate([q2 * low, q2 * high], axis=0)
        scores = dot_nt(stacked, k2) * (HD ** -0.5)
        if same_set is not None:
            scores = jnp.where(same_set, scores, -3e38)
        shifted = jnp.exp(scores - jnp.max(scores, axis=-1, keepdims=True))
        prob = shifted / jnp.sum(shifted, axis=-1, keepdims=True)
        probs[pair] = prob
        out = dot(prob.astype(BF), v2)
        mixed[:, cols] = jnp.where(is_low, out[:128], out[128:]).astype(BF)
        return carry

    lax.fori_loop(0, q.shape[1] // 128, pair_step, 0)


def attend_back(q, k, v, probs, gmix, gq, gk, gv):
    low, high, is_low = halves()

    def pair_step(pair, carry):
        cols = lanes(pair)
        q2, k2, v2, g2 = q[:, cols], k[:, cols], v[:, cols], gmix[:, cols]
        stacked = jnp.concatenate([q2 * low, q2 * high], axis=0)
        gstacked = jnp.concatenate([g2 * low, g2 * high], axis=0)
        prob = probs[pair]
        gprob = dot_nt(gstacked, v2)
        inner = jnp.sum(gprob * prob, axis=-1, keepdims=True)
        gscore = prob * (gprob - inner) * (HD ** -0.5)
        gv[:, cols] = dot_tn(prob.astype(BF), gstacked).astype(BF)
        gscore = gscore.astype(BF)
        out = dot(gscore, k2)
        gq[:, cols] = jnp.where(is_low, out[:128], out[128:]).astype(BF)
        gk[:, cols] = dot_tn(gscore, stacked).astype(BF)
        return carry

    lax.fori_loop(0, q.shape[1] // 128, pair_step, 0)


def wide_nt(base, pairs, out):
    def step(at, carry):
        cols = pl.ds(pl.multiple_of(at * 256, 256), 256)
        total = base[:, cols].astype(F32)
        for x, matrix, index in pairs:
            total = total + dot_nt(x[...], matrix[index, cols, :])
        out[:, cols] = total.astype(BF)
        return carry

    lax.fori_loop(0, out.shape[1] // 256, step, 0)


def put(units, group, product):
    for n in range(product.shape[1] // 128):
        part = product[:, 128 * n:128 * n + 128].astype(BF).reshape(-1, 16, 128)
        size = part.shape[0]
        units[pl.ds((group + n) * size, size)] = part


def wide_tn(left, right, units, group):
    def step(at, carry):
        cols = pl.ds(pl.multiple_of(at * 256, 256), 256)
        put(units, group + 2 * at, dot_tn(left[...], right[:, cols]))
        return carry

    lax.fori_loop(0, right.shape[1] // 256, step, 0)


class Sum:
    def __init__(self, place, g, sizes, blocks, paired, slots, part, slots2, own, slots3, row, fin,
                 ring, pair):
        self.place, self.g, self.sizes = place, g, sizes
        self.blocks, self.paired, self.slots, self.part = blocks, paired, slots, part
        self.slots2, self.own, self.slots3, self.row, self.fin = slots2, own, slots3, row, fin
        self.ring, self.pair = ring, pair
        self.offs = [sum(sizes[:k]) for k in range(3)]
        self.total = 16 * sum(sizes)

    def big(self, k, at, base=0):
        return pl.ds(base + 16 * self.offs[k] + at * (4 * self.sizes[k]), 4 * self.sizes[k])

    def small(self, k, at):
        return pl.ds(4 * self.offs[k] + at * self.sizes[k], self.sizes[k])

    def line(self, k):
        return pl.ds(4 * self.offs[k], 4 * self.sizes[k])

    def mine(self, k):
        return pl.ds(self.offs[k], self.sizes[k])

    def me(self, k, stage):
        return self.place[(k + stage) % 3]

    def peer(self, k, stage, at):
        x, y, z = self.place
        axis = (k + stage) % 3
        if axis == 0:
            return {"row": at * 2 + y % 2}
        if axis == 1:
            return {"row": x * 2 + at % 2, "col": (at // 2) * 4 + z}
        return {"col": (y // 2) * 4 + at}

    def copy(self, src, dst, sem, k, stage, slot_s, slot_r, at):
        return pltpu.make_async_remote_copy(
            src, dst, self.ring.at[sem, 0, k, slot_s], self.ring.at[sem, 1, k, slot_r],
            device_id=self.peer(k, stage, at), device_id_type=MESH,
        )

    def others(self, stage, step):
        def one(d, carry):
            for k in range(3):
                me = self.me(k, stage)
                step(k, me, (me + d % 3 + 1) % 4)
            return carry

        lax.fori_loop(1, 4, one, 0)

    def quarters(self, step):
        for k in range(3):
            def one(at, carry):
                step(k, at)
                return carry

            lax.fori_loop(0, 4, one, 0)

    def pair_copy(self, k, at):
        return pltpu.make_async_remote_copy(
            self.blocks.at[self.big(k, at, (1 - self.g) * self.total)],
            self.paired.at[self.big(k, at)],
            self.pair.at[0, 0, 4 * k + at], self.pair.at[0, 1, 4 * k + at],
            device_id={"grp": 1 - self.g}, device_id_type=MESH,
        )

    def pair_send(self):
        self.quarters(lambda k, at: self.pair_copy(k, at).start())

    def pair_add(self):
        def step(k, at):
            self.pair_copy(k, at).wait()
            some = self.big(k, at)
            total = self.blocks[self.big(k, at, self.g * self.total)].astype(F32)
            self.paired[some] = (total + self.paired[some].astype(F32)).astype(BF)

        self.quarters(step)

    def spread_copy(self, stage, k, me, at, arriving):
        slot = at if arriving else me
        if stage == 0:
            src, dst = self.paired.at[self.big(k, at)], self.slots.at[self.big(k, slot)]
        else:
            src, dst = self.part.at[self.small(k, at)], self.slots2.at[self.small(k, slot)]
        return self.copy(src, dst, stage, k, stage, at, slot, at)

    def spread_send(self, stage):
        self.others(
            stage, lambda k, me, at: self.spread_copy(stage, k, me, at, False).start()
        )

    def spread_add(self, stage):
        for k in range(3):
            me = self.me(k, stage)

            def one(d, carry):
                self.spread_copy(stage, k, me, (me + d) % 4, True).wait()
                return carry

            lax.fori_loop(1, 4, one, 0)
            if stage == 0:
                total = self.paired[self.big(k, me)].astype(F32)
                for d in range(1, 4):
                    total = total + self.slots[self.big(k, (me + d) % 4)].astype(F32)
                self.part[self.line(k)] = total.astype(BF)
            else:
                total = self.part[self.small(k, me)].astype(F32)
                for d in range(1, 4):
                    total = total + self.slots2[self.small(k, (me + d) % 4)].astype(F32)
                self.own[self.mine(k)] = total.astype(BF)

    def last_copy(self, k, me, at, arriving):
        slot = at if arriving else me
        dst = self.slots3.at[self.small(k, slot)]
        return self.copy(self.own.at[self.mine(k)], dst, 2, k, 2, at, slot, at)

    def last_send(self):
        self.others(2, lambda k, me, at: self.last_copy(k, me, at, False).start())

    def last_add(self):
        self.others(2, lambda k, me, at: self.last_copy(k, me, at, True).wait())
        for k in range(3):
            self.slots3[self.small(k, self.me(k, 2))] = self.own[self.mine(k)]
            total = self.slots3[self.small(k, 0)].astype(F32)
            for at in range(1, 4):
                total = total + self.slots3[self.small(k, at)].astype(F32)
            self.row[self.small(k, self.me(k, 1))] = total.astype(BF)

    def gather_copy(self, stage, k, me, at, arriving):
        slot = at if arriving else me
        if stage == 1:
            src, dst = self.row.at[self.small(k, me)], self.row.at[self.small(k, slot)]
        else:
            src = self.row.at[self.line(k)]
            dst = self.fin.at[self.big(k, slot, self.g * self.total)]
        return self.copy(src, dst, 4 - stage, k, stage, at, slot, at)

    def gather_send(self, stage):
        self.others(
            stage, lambda k, me, at: self.gather_copy(stage, k, me, at, False).start()
        )
        if stage == 0:
            for k in range(3):
                me = self.me(k, 0)
                self.fin[self.big(k, me, self.g * self.total)] = self.row[self.line(k)]
                self.over(k, me, True).start()

    def gather_wait(self, stage):
        def step(k, me, at):
            self.gather_copy(stage, k, me, at, True).wait()
            if stage == 0:
                self.over(k, at, True).start()

        self.others(stage, step)

    def over(self, k, at, mine):
        half = self.g if mine else 1 - self.g
        part = self.fin.at[self.big(k, at, half * self.total)]
        return pltpu.make_async_remote_copy(
            part, part, self.pair.at[1, 0, 4 * k + at], self.pair.at[1, 1, 4 * k + at],
            device_id={"grp": 1 - self.g}, device_id_type=MESH,
        )

    def pair_done(self):
        def step(k, at):
            self.over(k, at, True).wait_send()
            self.over(k, at, False).wait_recv()

        self.quarters(step)


class Loads:
    def __init__(self, copies):
        self.copies = copies

    def start(self):
        for copy in self.copies:
            copy.start()

    def wait(self):
        for copy in self.copies:
            copy.wait()


def cut_rows(ref, count):
    size = ref.shape[1] // count
    return [pl.ds(size * n, size) for n in range(count)]


def main_kernel(
    skip_hbm, grad_hbm, wup_hbm, win_hbm, wout_hbm, sw_hbm, tw_hbm,
    out, up_out, wide_out,
    skip, gpad, wup, win, wout, sw, tw,
    a1s, a1r, a2s, a2r, b1s, b1r, b2s, b2r, c1s, c1r, c2s, c2r, d1s, d1r, d2s, d2r,
    pooled_t, coarse_t, pooled_f, coarse_f, gunited, gexp, gexp_t, gtimed, gcoarse,
    qs, ks, vs, probs_s, qt, kt, vt, probs_t, mix, mix_t, attended, timed, gmix, gq, gk, gv, gatt,
    unit_t, skip_raw, grad_raw,
    x1, s1, z1, p1, t1, w1, v1, a1, fin1, x2, s2, z2, p2, t2, w2, v2, a2, fin2,
    load_sem, halo_sem, swap_sem, ring_sem1, pair_sem1, ring_sem2, pair_sem2,
):
    r, c, g = lax.axis_index("row"), lax.axis_index("col"), lax.axis_index("grp")
    frame_cuts = [pl.ds(8 * n, 8) for n in range(8)]
    loads = {}
    load_at = 0
    for name, pieces in (
        ("skip", [(skip_hbm.at[h], skip_raw.at[h]) for h in frame_cuts]),
        ("grad", [(grad_hbm.at[h], grad_raw.at[h]) for h in frame_cuts]),
        ("win", [(win_hbm, win)]),
        ("sw", [(sw_hbm.at[m, h], sw.at[m, h]) for m in range(4) for h in cut_rows(sw, 4)]),
        ("wout", [(wout_hbm, wout)]),
        ("tw", [(tw_hbm.at[m, h], tw.at[m, h]) for m in range(4) for h in cut_rows(tw, 4)]),
        ("wup", [(wup_hbm.at[m], wup.at[m]) for m in range(9)]),
    ):
        loads[name] = Loads(
            [pltpu.make_async_copy(src, dst, load_sem.at[load_at + n])
             for n, (src, dst) in enumerate(pieces)]
        )
        load_at += len(pieces)
    for name in ("skip", "grad", "win", "wup", "sw", "wout", "tw"):
        loads[name].start()

    around = [(dr, dc) for dr in (-1, 0, 1) for dc in (-1, 0, 1) if (dr, dc) != (0, 0)]

    def beside(dr, dc):
        return {"row": (r + dr + N) % N, "col": (c + dc + N) % N}

    barrier = pltpu.get_barrier_semaphore()
    for d in range(1, N):
        pl.semaphore_signal(barrier, 1, device_id={"row": (r + d) % N}, device_id_type=MESH)
        pl.semaphore_signal(barrier, 1, device_id={"col": (c + d) % N}, device_id_type=MESH)
    for dr, dc in around:
        if dr != 0 and dc != 0:
            pl.semaphore_signal(barrier, 1, device_id=beside(dr, dc), device_id_type=MESH)
    x, y, z = r // 2, (c // 4) * 2 + r % 2, c % 4
    pl.semaphore_signal(
        barrier, 1, device_id={"row": x * 2 + (r + 1) % 2, "col": (c + 4) % N}, device_id_type=MESH
    )
    pl.semaphore_signal(barrier, 1, device_id={"grp": 1 - g}, device_id_type=MESH)
    first = Sum(
        (x, y, z), g, SIZES1, x1, s1, z1, p1, t1, w1, v1, a1, fin1, ring_sem1, pair_sem1
    )
    second = Sum(
        (x, y, z), g, SIZES2, x2, s2, z2, p2, t2, w2, v2, a2, fin2, ring_sem2, pair_sem2
    )

    def send(stage, src, dst, axis, me):
        dst[me] = src[me]

        def step(d, carry):
            peer = (me + d) % N
            pltpu.make_async_remote_copy(
                src.at[peer], dst.at[me], swap_sem.at[stage, 0, peer], swap_sem.at[stage, 1, me],
                device_id={axis: peer}, device_id_type=MESH,
            ).start()
            return carry

        lax.fori_loop(1, N, step, 0)

    def arrive(stage, src, dst, axis, me):
        def step(d, carry):
            peer = (me + d) % N
            pltpu.make_async_remote_copy(
                src.at[peer], dst.at[peer], swap_sem.at[stage, 0, peer], swap_sem.at[stage, 1, peer],
                device_id={axis: peer}, device_id_type=MESH,
            ).wait()
            return carry

        lax.fori_loop(1, N, step, 0)

    def turn(src, dst, back):
        width = src.shape[2]
        rows = src[...].reshape(128, width)
        dst[...] = dot(permutation(back), rows).astype(BF).reshape(N, 16, width)

    def halo(k):
        dr, dc = around[k]
        src = gpad.at[
            {-1: pl.ds(1, 1), 0: pl.ds(1, 8), 1: pl.ds(8, 1)}[dr],
            {-1: pl.ds(1, 1), 0: pl.ds(1, 4), 1: pl.ds(4, 1)}[dc],
        ]
        dst = gpad.at[
            {-1: pl.ds(9, 1), 0: pl.ds(1, 8), 1: pl.ds(0, 1)}[dr],
            {-1: pl.ds(5, 1), 0: pl.ds(1, 4), 1: pl.ds(0, 1)}[dc],
        ]
        return pltpu.make_async_remote_copy(
            src, dst, halo_sem.at[0, k], halo_sem.at[1, k],
            device_id=beside(dr, dc), device_id_type=MESH,
        )

    def halo_each(k, way, act):
        tests = [
            {-1: at > 0, 1: at < N - 1}[way * d]
            for at, d in zip((r, c), around[k]) if d != 0
        ]

        @pl.when(tests[0] if len(tests) == 1 else jnp.logical_and(*tests))
        def _():
            act(halo(k))

    loads["skip"].wait()
    for i in range(8):
        skip[i] = jnp.swapaxes(skip_raw[:, i], 0, 1)
    means = []
    for p in range(2):
        total = jnp.zeros(skip.shape[2:], F32)
        for i in range(POOL):
            for j in range(POOL):
                total = total + skip[p * POOL + i, j].astype(F32)
        means.append(total * (1.0 / (POOL * POOL)))
    for f in range(N):
        rows = jnp.concatenate([means[0][8 * f:8 * f + 8], means[1][8 * f:8 * f + 8]], axis=0)
        a1s[f] = rows.astype(BF)
    pooled_t[...] = a1s[...].reshape(128, -1)
    loads["grad"].wait()
    for i in range(8):
        gpad[1 + i, 1:5] = jnp.swapaxes(grad_raw[:, i], 0, 1)
    pl.semaphore_wait(barrier, 2 * (N - 1) + 6)
    send(0, a1s, a1r, "row", r)
    x1[660:] = jnp.zeros((12,) + x1.shape[1:], BF)
    x2[200:] = jnp.zeros((24,) + x2.shape[1:], BF)
    loads["win"].wait()
    coarse_t[...] = dot(pooled_t[...], win[...]).astype(BF)
    chan = gpad.shape[3]
    def tap_rows(tap, cols):
        dy, dx = tap // 3, tap % 3
        return gpad[pl.ds(2 - dy, 8), pl.ds(2 - dx, 4), :, cols].reshape(2048, -1)

    def tap_step(tap, carry):
        put(x1, 2 * tap, dot(unit_t[...], tap_rows(tap, slice(0, 256))))
        return carry

    def weight_taps(first_tap, last_tap):
        lax.fori_loop(first_tap, last_tap, tap_step, 0)

    def back_taps(rows_of, size):
        total = jnp.zeros((size, chan), F32)
        for dy in range(3):
            for dx in range(3):
                total = total + dot_nt(rows_of(dy, dx).reshape(size, chan), wup[3 * dy + dx])
        return total.astype(BF)

    def back_inner(p):
        low = back_taps(lambda dy, dx: gpad[3 * p + 3 - dy:3 * p + 6 - dy, 3 - dx:5 - dx], 384)
        low = low.reshape(3, 2, 64, chan)
        gunited[3 * p + 1:3 * p + 4, 1:3] = low
        gexp[p] = jnp.sum(low.astype(F32), axis=(0, 1))

    def back_sides(p, carry):
        def rows_of(dy, dx):
            near = pl.ds(3 * p + 3 - dy, 3)
            return jnp.concatenate([gpad[near, 2 - dx], gpad[near, 5 - dx]], axis=0)

        low = back_taps(rows_of, 384).reshape(2, 3, 64, chan)
        gunited[pl.ds(3 * p + 1, 3), 0] = low[0]
        gunited[pl.ds(3 * p + 1, 3), 3] = low[1]
        gexp[p] += jnp.sum(low.astype(F32), axis=(0, 1))
        return carry

    def back_ends(p, carry):
        low = back_taps(lambda dy, dx: gpad[7 * p + 2 - dy, 2 - dx:6 - dx], 256)
        low = low.reshape(4, 64, chan)
        gunited[7 * p] = low
        gexp[p] += jnp.sum(low.astype(F32), axis=0)
        return carry

    loads["wup"].wait()
    back_inner(0)
    arrive(0, a1s, a1r, "row", r)
    turn(a1r, a2s, False)
    send(1, a2s, a2r, "col", c)
    back_inner(1)
    arrive(1, a2s, a2r, "col", c)
    for k in (3, 4):
        halo_each(k, 1, lambda copy: copy.start())
    pooled_f[...] = a2r[...].reshape(128, chan)

    coarse_f[...] = dot(pooled_f[...], win[...]).astype(BF)
    loads["sw"].wait()
    for m, ref in enumerate((qs, ks, vs)):
        ref[...] = dot(coarse_f[...], sw[m]).astype(BF)
    attend(qs, ks, vs, probs_s, mix, None)
    b1s[...] = mix[...].reshape(b1s.shape)
    send(2, b1s, b1r, "col", c)
    arrive(2, b1s, b1r, "col", c)
    turn(b1r, b2s, True)
    send(3, b2s, b2r, "row", r)
    for k in (1, 6, 0, 2, 5, 7):
        halo_each(k, 1, lambda copy: copy.start())
    arrive(3, b2s, b2r, "row", r)
    mix_t[...] = b2r[...].reshape(mix_t.shape)

    loads["wout"].wait()
    loads["tw"].wait()
    wide_nt(coarse_t, [(mix_t, sw, 3)], attended)
    for m, ref in enumerate((qt, kt, vt)):
        ref[...] = dot(attended[...], tw[m]).astype(BF)
    row_pixel = lax.broadcasted_iota(jnp.int32, (256, 128), 0) % 16 // 8
    key_pixel = lax.broadcasted_iota(jnp.int32, (256, 128), 1) % 16 // 8
    attend(qt, kt, vt, probs_t, mix, row_pixel == key_pixel)
    wide_nt(attended, [(mix, tw, 3)], timed)
    expanded = dot_nt(timed[...], wout[...])
    for p in range(2):
        rows = jnp.concatenate(
            [expanded[16 * f + 8 * p:16 * f + 8 * p + 8] for f in range(N)], axis=0
        )

        def unite(i, carry):
            united = (skip[i].astype(F32) + rows[None]).astype(BF).reshape(256, chan)
            unit_t[:, pl.ds(pl.multiple_of(i * 256, 256), 256)] = united.T
            return carry

        lax.fori_loop(p * POOL, p * POOL + POOL, unite, 0)
    for k in range(8):
        halo_each(k, 1, lambda copy: copy.wait_send())
        halo_each(k, -1, lambda copy: copy.wait_recv())

    @pl.when(r == 0)
    def _():
        gpad[0] = jnp.zeros(gpad.shape[1:], BF)

    @pl.when(r == N - 1)
    def _():
        gpad[9] = jnp.zeros(gpad.shape[1:], BF)

    @pl.when(c == 0)
    def _():
        gpad[:, 0] = jnp.zeros((10,) + gpad.shape[2:], BF)

    @pl.when(c == N - 1)
    def _():
        gpad[:, 5] = jnp.zeros((10,) + gpad.shape[2:], BF)

    lax.fori_loop(0, 2, back_sides, 0)
    lax.fori_loop(0, 2, back_ends, 0)
    for f in range(N):
        rows = jnp.concatenate([gexp[0, 8 * f:8 * f + 8], gexp[1, 8 * f:8 * f + 8]], axis=0)
        gexp_t[16 * f:16 * f + 16] = rows.astype(BF)
    gtimed[...] = dot(gexp_t[...], wout[...]).astype(BF)
    gmix[...] = dot(gtimed[...], tw[3]).astype(BF)
    attend_back(qt, kt, vt, probs_t, gmix, gq, gk, gv)
    wide_nt(gtimed, [(gq, tw, 0), (gk, tw, 1), (gv, tw, 2)], gatt)
    c1s[...] = gatt[...].reshape(c1s.shape)
    send(4, c1s, c1r, "row", r)

    wide_tn(gexp_t, timed, x1, 23)
    weight_taps(0, 5)
    arrive(4, c1s, c1r, "row", r)
    turn(c1r, c2s, False)
    send(5, c2s, c2r, "col", c)

    weight_taps(5, 9)
    for taps, at in (((0, 1, 2, 3), 18), ((4, 5, 6, 7), 20)):
        rows = jnp.concatenate([tap_rows(tap, slice(256, chan)) for tap in taps], axis=1)
        put(x1, at, dot(unit_t[...], rows))
    rows = jnp.concatenate([tap_rows(8, slice(256, chan))] * 2, axis=1)
    put(x1, 22, dot(unit_t[...], rows))
    first.pair_send()
    arrive(5, c2s, c2r, "col", c)
    gatt[...] = c2r[...].reshape(gatt.shape)

    gmix[...] = dot(gatt[...], sw[3]).astype(BF)
    first.pair_add()
    first.spread_send(0)
    attend_back(qs, ks, vs, probs_s, gmix, gq, gk, gv)
    wide_nt(gatt, [(gq, sw, 0), (gk, sw, 1), (gv, sw, 2)], gcoarse)
    wide_tn(pooled_f, gcoarse, x2, 0)
    second.pair_send()
    d1s[...] = dot_nt(gcoarse[...], win[...]).astype(BF).reshape(d1s.shape)
    first.spread_add(0)
    first.spread_send(1)
    send(6, d1s, d1r, "col", c)
    second.pair_add()
    second.spread_send(0)
    first.spread_add(1)
    first.last_send()
    arrive(6, d1s, d1r, "col", c)
    turn(d1r, d2s, True)
    send(7, d2s, d2r, "row", r)
    first.last_add()
    first.gather_send(1)
    second.spread_add(0)
    second.spread_send(1)
    first.gather_wait(1)
    first.gather_send(0)
    second.spread_add(1)
    second.last_send()
    arrive(7, d2s, d2r, "row", r)
    spread = d2r[...].reshape(128, chan).astype(F32) * (1.0 / (POOL * POOL))
    for p in range(2):
        rows = jnp.concatenate(
            [spread[16 * f + 8 * p:16 * f + 8 * p + 8] for f in range(N)], axis=0
        )

        def finish(i, carry):
            full = (gunited[i].astype(F32) + rows[None]).astype(BF)
            skip_raw[:, i] = jnp.swapaxes(full, 0, 1)
            return carry

        lax.fori_loop(p * POOL, p * POOL + POOL, finish, 0)
    stores = Loads([
        pltpu.make_async_copy(skip_raw.at[h], out.at[h], load_sem.at[n])
        for n, h in enumerate(frame_cuts)
    ])
    stores.start()
    second.last_add()
    second.gather_send(1)
    second.gather_wait(1)
    second.gather_send(0)
    first.gather_wait(0)
    second.gather_wait(0)
    first.pair_done()

    def group_of(fin, at):
        return fin[pl.ds(20 * at, 20)].reshape(chan, 128)

    def whole(at, carry):
        up_out[at // 2, :, lanes(at % 2)] = group_of(fin1, at)
        return carry

    lax.fori_loop(0, 18, whole, 0)
    for at in range(5):
        rest = group_of(fin1, 18 + at)
        up_out[2 * at, :, 256:chan] = rest[:, :chan - 256]
        if at < 4:
            up_out[2 * at + 1, :, 256:chan] = rest[:, chan - 256:]

    def wide_group(at, carry):
        wide_out[0, :, lanes(at)] = group_of(fin1, 23 + at)
        return carry

    lax.fori_loop(0, 10, wide_group, 0)
    second.pair_done()

    def wide_group2(at, carry):
        wide_out[1, :, lanes(at)] = group_of(fin2, at)
        return carry

    lax.fori_loop(0, 10, wide_group2, 0)
    stores.wait()


def shards(skip, w_up, w_in, w_out, spatial_w, temporal_w, grad_out):
    frames, tile_h, tile_w, chan = skip.shape
    wide = w_in.shape[1]
    att = spatial_w.shape[2]
    skip_shape = (tile_h, tile_w, frames, chan)
    w_out_t = w_out.T

    def vm(shape, dtype=BF):
        return pltpu.VMEM(shape, dtype)

    tok = 128
    swaps = []
    for width in (chan, att, wide, chan):
        swaps += [vm((N, 16, width))] * 4

    def sums(sizes):
        u = sum(sizes)
        return [vm((n * u, 16, 128)) for n in (32, 16, 16, 4, 4, 1, 4, 4, 32)]

    scratch = [
        vm(skip_shape), vm((tile_h + 2, tile_w + 2, frames, chan)), vm(w_up.shape),
        vm(w_in.shape), vm(w_out_t.shape), vm(spatial_w.shape), vm(temporal_w.shape),
        *swaps,
        vm((tok, chan)), vm((tok, wide)), vm((tok, chan)), vm((tok, wide)),
        vm(skip_shape), vm((2, frames, chan), F32), vm((tok, chan)), vm((tok, wide)),
        vm((tok, wide)),
        vm((tok, att)), vm((tok, att)), vm((tok, att)), vm((att // 128, 256, 128), F32),
        vm((tok, att)), vm((tok, att)), vm((tok, att)), vm((att // 128, 256, 128), F32),
        vm((tok, att)), vm((tok, att)), vm((tok, wide)), vm((tok, wide)),
        vm((tok, att)), vm((tok, att)), vm((tok, att)), vm((tok, att)), vm((tok, wide)),
        vm((chan, frames * tile_h * tile_w)),
        vm(skip.shape), vm(skip.shape),
        *sums(SIZES1), *sums(SIZES2),
        pltpu.SemaphoreType.DMA((59,)), pltpu.SemaphoreType.DMA((2, 8)),
        pltpu.SemaphoreType.DMA((8, 2, N)),
        *[pltpu.SemaphoreType.DMA((5, 2, 3, 4)), pltpu.SemaphoreType.DMA((2, 2, 12))] * 2,
    ]
    grad_skip, up, wide_grads = pl.pallas_call(
        main_kernel,
        out_shape=(
            jax.ShapeDtypeStruct(skip.shape, BF),
            jax.ShapeDtypeStruct(w_up.shape, BF),
            jax.ShapeDtypeStruct((2,) + w_in.shape, BF),
        ),
        in_specs=[pl.BlockSpec(memory_space=pl.ANY)] * 7,
        out_specs=[pl.BlockSpec(memory_space=pl.ANY)] + [pl.BlockSpec(memory_space=pltpu.VMEM)] * 2,
        scratch_shapes=scratch,
        compiler_params=pltpu.CompilerParams(
            collective_id=0, has_side_effects=True, vmem_limit_bytes=60 * 1024 * 1024
        ),
        name="backward",
    )(skip, grad_out, w_up, w_in, w_out_t, spatial_w, temporal_w)
    grad_w_out, grad_w_in = wide_grads[0].astype(F32).T, wide_grads[1].astype(F32)
    return (grad_skip, up.astype(F32), grad_w_in, grad_w_out)


def solution(mesh):
    in_specs = (P("grp", "row", "col", None), P(), P(), P(), P(), P(), P("grp", "row", "col", None))
    out_specs = (P("grp", "row", "col", None), P(), P(), P())
    return jax.shard_map(shards, mesh=mesh, in_specs=in_specs, out_specs=out_specs, check_vma=False)
```
